256 devices in a mesh: replica: 32 (over x_hi, z, core), fsdp: 8 (over x_lo, y).
Axes of the slice: x: 4 (x_hi: 2, x_lo: 2; x = x_hi * 2 + x_lo), y: 4, z: 8, core: 2. Of those that a mesh axis runs over, the one named last changes fastest.
Arguments:
- tokens: bfloat16 [163840, 4096], P(('replica', 'fsdp')), may hold values from -6 to 6
- cotangent: bfloat16 [163840, 512], P(('replica', 'fsdp')), may hold values from -6 to 6
- momentum: float32 [32, 4096, 512], P('replica', 'fsdp'), may hold values from -24 to 24
- kept_index: int32 [32, 8, 32768], P(None, None, 'fsdp'), may hold values from 0 to 63, as said below
Outputs:
- new_momentum: float32 [32, 4096, 512], P('replica', 'fsdp')
- update: float32 [4096, 512], P('fsdp')
The draws below stay inside these ranges and needn't reach their ends.
Inputs may be any that keep to these rules, and one draw needn't show every extreme that they name: `kept_index`: for each replica and block the 8 frequencies are distinct.
All inputs are finite; a program needn't handle non-finite values.
Results may differ from the reference program's by a relative error of at most 0.0003.
Values sent between devices are 32-bit elements; how exact they have to be, the bound alone decides.
No kernel may reach another device: no remote copies, remote signals or barrier semaphores. Data moves between devices by JAX's collectives and lax.ppermute only.
A program may use at most 128 MiB of HBM per device.

```python
import math
import jax
import jax.numpy as jnp
from jax import lax

D = 4096
DK = 512
BLOCK = 64
KEEP = 8
TOK_DEV = 640
TOKENS = 163840
BLOCKS = 32768
N_REPLICA = 32
N_FSDP = 8


def draw_kept_index(key, part):
    key = jax.random.fold_in(key, 7)
    shape = (N_REPLICA, BLOCKS, BLOCK)
    scores = jax.random.randint(key, shape, 0, 1 << 20, dtype=jnp.int32) * BLOCK + lax.broadcasted_iota(jnp.int32, shape, 2)
    ranking = jnp.argsort(scores, axis=2)
    return jnp.transpose(ranking[:, :, :KEEP], (0, 2, 1)).astype(jnp.int32)


def steps_of(key, extent, split, least, high):
    factor_of = 1.0
    for dim, parts in split:
        draws = jax.random.uniform(jax.random.fold_in(jax.random.fold_in(key, 6), dim), (parts,), jnp.float32, least / len(split), high / len(split))
        factor_of = factor_of * jnp.repeat(jnp.exp(draws), extent[dim] // parts).reshape((-1,) + (1,) * (len(extent) - 1 - dim))
    return factor_of


def normal_values(own_key, shape, width, bound, split=(), held_as=jnp.bfloat16):
    drawn = width * jax.random.normal(own_key, shape, jnp.float32)
    if split:
        drawn = drawn * steps_of(own_key, shape, split, -0.22, 0.18)
    return jnp.clip(drawn, -bound, bound).astype(held_as)


def setup_inputs(seed: int = 0) -> dict:
    keys = jax.random.split(jax.random.key(seed), 5)
    return {
        "tokens": normal_values(keys[0], (TOKENS, D), 1.0, 6.0, ((0, 256),)),
        "cotangent": normal_values(keys[1], (TOKENS, DK), 1.0, 6.0, ((0, 256),)),
        "momentum": normal_values(keys[2], (N_REPLICA, D, DK), 4.0, 24.0, ((0, 32), (1, 8)), jnp.float32),
        "kept_index": draw_kept_index(jax.random.fold_in(keys[4], 71), 0),
    }


momentum_decay = 0.9

def cosines(length):
    frequency = lax.broadcasted_iota(jnp.float32, (length, length), 0)
    position = lax.broadcasted_iota(jnp.float32, (length, length), 1)
    factor = jnp.where(frequency == 0.0, math.sqrt(1.0 / length), math.sqrt(2.0 / length))
    return factor * jnp.cos(math.pi * (2.0 * position + 1.0) * frequency / (2.0 * length))

def forward(weights, cosine_rows):
    length = cosine_rows.shape[0]
    blocks = weights.reshape(weights.shape[0], weights.shape[1] // length, length)
    spectra = jnp.einsum('rbn,kn->krb', blocks, cosine_rows, precision=lax.Precision.HIGHEST)
    return spectra.reshape(length, -1)

def inverse(spectra, cosine_rows, row_width):
    length = cosine_rows.shape[0]
    spectral_grid = spectra.reshape(length, -1, row_width // length)
    rebuilt = jnp.einsum('krb,kn->rbn', spectral_grid, cosine_rows, precision=lax.Precision.HIGHEST)
    return rebuilt.reshape(-1, row_width)

def reference(tokens, cotangent, momentum, kept_index):
    cosine_rows = cosines(BLOCK)
    tokens_all = tokens.reshape(N_REPLICA, N_FSDP, TOK_DEV, D)
    cotangent_all = cotangent.reshape(N_REPLICA, N_FSDP, TOK_DEV, DK)
    factor = 1.0 / math.sqrt(TOK_DEV * N_FSDP)
    columns_all = jnp.arange(BLOCKS, dtype=jnp.int32)

    def add_term(running, couple):
        partial_value = jnp.dot(couple[0].T, couple[1], preferred_element_type=jnp.float32)
        return (running + partial_value, None)

    def one_replica(running_update, member):
        tokens_rep, cotangent_rep, momentum_rep, chosen = member
        summed, _ = lax.scan(add_term, jnp.zeros((D, DK), jnp.float32), (tokens_rep, cotangent_rep))
        moment = momentum_decay * momentum_rep + factor * summed
        spectra = forward(moment, cosine_rows)
        kept = jnp.take_along_axis(spectra, chosen, axis=0)
        filled = jnp.zeros((BLOCK, BLOCKS), jnp.float32).at[chosen, columns_all[None, :]].set(kept)
        rebuilt = inverse(filled, cosine_rows, DK)
        return (running_update + rebuilt, moment - rebuilt)
    summed_update, new_momentum = lax.scan(one_replica, jnp.zeros((D, DK), jnp.float32), (tokens_all, cotangent_all, momentum, kept_index))
    return (new_momentum, summed_update / N_REPLICA)
```

```python
import functools
import math

import jax
import jax.numpy as jnp
import numpy as np
from jax import lax
from jax.experimental import pallas as pl
from jax.experimental.pallas import tpu as pltpu
from jax.sharding import PartitionSpec as P

BLOCK = 64
KEEP = 8
UNIT = 128
DECAY = 0.9
HIGHEST = lax.Precision.HIGHEST


def paired_cosines():
    k = np.arange(BLOCK, dtype=np.float64)[:, None]
    n = np.arange(BLOCK, dtype=np.float64)[None, :]
    c = np.sqrt(np.where(k == 0, 1.0, 2.0) / BLOCK) * np.cos(np.pi * (2 * n + 1) * k / (2 * BLOCK))
    both = np.zeros((2 * BLOCK, 2 * BLOCK))
    both[:BLOCK, :BLOCK] = c
    both[BLOCK:, BLOCK:] = c
    return both.astype(np.float32)


def products(tokens, cotangent, table, groups, addends):
    depth, width = cotangent.shape
    units = [u for group in groups for u in group]
    extra = [item for group in addends for item in group]
    counts = [len(group) for group in addends]

    def kernel(table_ref, *refs):
        token_refs = refs[: len(units)]
        cot_ref = refs[len(units)]
        extra_refs = refs[len(units) + 1 : len(units) + 1 + len(extra)]
        out_refs = refs[len(units) + 1 + len(extra) :]
        at = 0
        first = 0
        for g, group in enumerate(groups):
            for m in range(len(group)):
                value = lax.dot_general(
                    token_refs[at][...],
                    cot_ref[...],
                    (((0,), (0,)), ((), ())),
                    preferred_element_type=jnp.float32,
                )
                rows = slice(m * UNIT, (m + 1) * UNIT)
                for e in range(counts[g]):
                    value = value + extra_refs[first + e][rows, :]
                out_refs[g][rows, :] = value
                at += 1
            first += counts[g]

    in_specs = [pl.BlockSpec((depth, UNIT), lambda i, t, m=m: (0, t[m])) for m in range(len(units))]
    in_specs.append(pl.BlockSpec((depth, width), lambda i, t: (0, 0)))
    for g, group in enumerate(addends):
        size = UNIT * len(groups[g])
        for _, start in group:
            in_specs.append(pl.BlockSpec((size, width), lambda i, t, s=start // len(groups[g]): (s, 0)))
    outs = [jax.ShapeDtypeStruct((UNIT * len(group), width), jnp.float32) for group in groups]
    flops = 2 * depth * UNIT * width * len(units)
    moved = len(units) * (depth * UNIT * 2 + UNIT * width * 4) + depth * width * 2 + len(extra) * UNIT * width * 4
    return pl.pallas_call(
        kernel,
        out_shape=outs,
        grid_spec=pltpu.PrefetchScalarGridSpec(
            num_scalar_prefetch=1,
            grid=(1,),
            in_specs=in_specs,
            out_specs=[pl.BlockSpec(o.shape, lambda i, t: (0, 0)) for o in outs],
        ),
        compiler_params=pltpu.CompilerParams(vmem_limit_bytes=24 << 20),
        cost_estimate=pl.CostEstimate(flops=flops, bytes_accessed=moved, transcendentals=0),
    )(jnp.stack([table[u] for u in units]), *([tokens] * len(units)), cotangent, *[a for a, _ in extra])


def project(summed, momentum, first, factor, chosen, cosine_pair):
    rows, width = summed[0].shape
    pairs = width // (2 * BLOCK)
    parts = len(summed)

    def kernel(*refs):
        part_refs = refs[:parts]
        momentum_ref, chosen_ref, cos_ref, kept_ref, rest_ref = refs[parts:]
        total = part_refs[0][...]
        for ref in part_refs[1:]:
            total = total + ref[...]
        moment = DECAY * momentum_ref[...] + factor * total
        cos = cos_ref[...]
        frequency = lax.broadcasted_iota(jnp.int32, (BLOCK, rows), 0)
        for g in range(pairs):
            columns = slice(2 * BLOCK * g, 2 * BLOCK * (g + 1))
            spectrum = lax.dot_general(
                cos, moment[:, columns], (((1,), (1,)), ((), ())), precision=HIGHEST, preferred_element_type=jnp.float32
            )
            masked = []
            for half in range(2):
                own = spectrum[half * BLOCK : (half + 1) * BLOCK]
                filled = jnp.zeros_like(own)
                for j in range(KEEP):
                    line = j * 2 * pairs + 2 * g + half
                    hit = frequency == chosen_ref[line : line + 1, :]
                    taken = jnp.where(hit, own, 0.0)
                    kept_ref[line : line + 1, :] = jnp.sum(taken, axis=0, keepdims=True)
                    filled = filled + taken
                masked.append(filled)
            rebuilt = lax.dot_general(
                jnp.concatenate(masked, axis=0), cos, (((0,), (0,)), ((), ())), precision=HIGHEST,
                preferred_element_type=jnp.float32,
            )
            rest_ref[:, columns] = moment[:, columns] - rebuilt

    lines = KEEP * 2 * pairs
    full = lambda i: (0, 0)
    return pl.pallas_call(
        kernel,
        out_shape=[
            jax.ShapeDtypeStruct((lines, rows), jnp.float32),
            jax.ShapeDtypeStruct((rows, width), jnp.float32),
        ],
        grid=(1,),
        in_specs=[pl.BlockSpec((rows, width), full)] * parts
        + [
            pl.BlockSpec((rows, width), lambda i: (first // rows, 0)),
            pl.BlockSpec((lines, rows), lambda i: (0, first // rows)),
            pl.BlockSpec(cosine_pair.shape, full),
        ],
        out_specs=[pl.BlockSpec((lines, rows), full), pl.BlockSpec((rows, width), full)],
        compiler_params=pltpu.CompilerParams(vmem_limit_bytes=24 << 20),
        cost_estimate=pl.CostEstimate(flops=rows * 2000000, bytes_accessed=rows * width * 4 * (parts + 2), transcendentals=0),
    )(*summed, momentum, chosen, cosine_pair)


def spread(values, chosen, order, first, cosine_pair, scale):
    lines, rows = values[0].shape
    members = len(values)
    width = lines // KEEP * BLOCK
    pairs = width // (2 * BLOCK)

    def kernel(order_ref, *refs):
        value_refs = refs[:members]
        chosen_ref, cos_ref, out_ref = refs[members:]
        cos = cos_ref[...]
        frequency = lax.broadcasted_iota(jnp.int32, (BLOCK, rows), 0)
        for g in range(pairs):
            filled = []
            for half in range(2):
                total = jnp.zeros((BLOCK, rows), jnp.float32)
                for m in range(members):
                    own = jnp.zeros((BLOCK, rows), jnp.float32)
                    for j in range(KEEP):
                        line = j * 2 * pairs + 2 * g + half
                        hit = frequency == chosen_ref[order_ref[m], line : line + 1, :]
                        own = jnp.where(hit, value_refs[m][line : line + 1, :], own)
                    total = total + own
                filled.append(total)
            out_ref[:, 2 * BLOCK * g : 2 * BLOCK * (g + 1)] = scale * lax.dot_general(
                jnp.concatenate(filled, axis=0), cos, (((0,), (0,)), ((), ())), precision=HIGHEST,
                preferred_element_type=jnp.float32,
            )

    return pl.pallas_call(
        kernel,
        out_shape=jax.ShapeDtypeStruct((rows, width), jnp.float32),
        grid_spec=pltpu.PrefetchScalarGridSpec(
            num_scalar_prefetch=1,
            grid=(1,),
            in_specs=[pl.BlockSpec((lines, rows), lambda i, t: (0, 0))] * members
            + [
                pl.BlockSpec((members, lines, rows), lambda i, t: (0, 0, first // rows)),
                pl.BlockSpec(cosine_pair.shape, lambda i, t: (0, 0)),
            ],
            out_specs=pl.BlockSpec((rows, width), lambda i, t: (0, 0)),
        ),
        compiler_params=pltpu.CompilerParams(vmem_limit_bytes=24 << 20),
        cost_estimate=pl.CostEstimate(flops=rows * 10000000, bytes_accessed=rows * width * 8, transcendentals=0),
    )(order, *values, chosen, cosine_pair)


def on_device(tokens, cotangent, momentum, kept_index):
    nx, ny = 2, 4
    nh, nz, nc = 2, 8, 2
    width = cotangent.shape[1]
    blocks_in_row = width // BLOCK
    rows = momentum.shape[1]
    chunks = rows // UNIT
    group_size = lax.axis_size("fsdp")
    replicas = lax.axis_size("replica")
    factor = 1.0 / math.sqrt(tokens.shape[0] * group_size)
    cosine_pair = jnp.asarray(paired_cosines())

    f = lax.axis_index("fsdp")
    x, y = f // ny, f % ny
    r = lax.axis_index("replica")
    h, z, c = r // (nz * nc), r // nc % nz, r % nc

    up = [(i, i // ny * ny + (i + 1) % ny) for i in range(nx * ny)]
    down = [(i, i // ny * ny + (i - 1) % ny) for i in range(nx * ny)]
    across = [(i, (i + ny) % (nx * ny)) for i in range(nx * ny)]
    to_up = lambda v: lax.ppermute(v, "fsdp", up)
    to_down = lambda v: lax.ppermute(v, "fsdp", down)
    to_across = lambda v: lax.ppermute(v, "fsdp", across)

    def along(d):
        return [(i, i // (nz * nc) * (nz * nc) + ((i // nc + d) % nz) * nc + i % nc) for i in range(nh * nz * nc)]

    table = {
        (dx, dy, k): ((x + dx) % nx * ny + (y + dy) % ny) * chunks + k
        for dx in range(nx)
        for dy in range(ny)
        for k in range(chunks)
    }
    make = functools.partial(products, tokens, cotangent, table)

    grouped = kept_index.reshape(nh, nz, nc, KEEP, -1)
    grouped = lax.dynamic_slice(grouped, (h, 0, c, 0, 0), (1, nz, 1, KEEP, grouped.shape[-1]))
    chosen = grouped.reshape(nz, KEEP, rows, blocks_in_row).transpose(0, 1, 3, 2).reshape(nz, KEEP * blocks_in_row, rows)
    own_chosen = lax.dynamic_index_in_dim(chosen, z, 0, keepdims=False)
    order = jnp.stack([(z - d) % nz for d in range(nz)]).astype(jnp.int32)

    def y_first(k):
        far = make([[(0, 2, k)], [(1, 2, k)]], [[], []])
        a1, b1 = to_up(far[0]), to_down(far[1])
        near = make([[(1, 1, k)], [(0, 3, k)]], [[], []])
        a2, b2 = to_up(near[0]), to_down(near[1])
        last = make([[(0, 1, k)], [(1, 3, k)]], [[(a1, 0)], [(b1, 0)]])
        a3, b3 = to_up(last[0]), to_down(last[1])
        (other,) = make([[(1, 0, k)]], [[(a2, 0), (b3, 0)]])
        received = to_across(other)
        (own,) = make([[(0, 0, k)]], [[(a3, 0), (b2, 0)]])
        return [own, received]

    def x_first(ka, kb):
        x2 = to_across(make([[(1, 2, ka), (1, 2, kb)]], [[]])[0])
        x1 = to_across(make([[(1, 1, kb), (1, 3, ka)]], [[]])[0])
        x3 = to_across(make([[(1, 1, ka), (1, 3, kb)]], [[]])[0])
        x0 = to_across(make([[(1, 0, ka), (1, 0, kb)]], [[]])[0])
        far = make([[(0, 2, ka)], [(0, 2, kb)]], [[(x2, 0)], [(x2, 1)]])
        a1, b1 = to_up(far[0]), to_down(far[1])
        near = make([[(0, 1, kb)], [(0, 3, ka)]], [[(x1, 0)], [(x1, 1)]])
        a2, b2 = to_up(near[0]), to_down(near[1])
        last = make([[(0, 1, ka)], [(0, 3, kb)]], [[(x3, 0), (a1, 0)], [(x3, 1), (b1, 0)]])
        a3, b3 = to_up(last[0]), to_down(last[1])
        own = make([[(0, 0, ka)], [(0, 0, kb)]], [[(x0, 0)], [(x0, 1)]])
        return [own[0], a3, b2], [own[1], a2, b3]

    def gather(kept):
        return [kept] + [lax.ppermute(kept, "replica", along(d)) for d in range(1, nz)]

    swap_core = [(i, i ^ 1) for i in range(nh * nz * nc)]
    swap_half = [(i, (i + nz * nc) % (nh * nz * nc)) for i in range(nh * nz * nc)]

    rest = [None] * chunks
    update = [None] * chunks
    parts = [None] * chunks
    parts[0] = y_first(0)
    parts[2], parts[3] = x_first(2, 3)
    parts[1] = y_first(1)
    for k in (0, 2, 3, 1):
        kept, rest[k] = project(parts[k], momentum[0], k * UNIT, factor, own_chosen, cosine_pair)
        dense = spread(gather(kept), chosen, order, k * UNIT, cosine_pair, 1.0 / replicas)
        dense = dense + lax.ppermute(dense, "replica", swap_core)
        update[k] = dense + lax.ppermute(dense, "replica", swap_half)
    return jnp.concatenate(rest, 0)[None], jnp.concatenate(update, 0)


def solution(mesh):
    in_specs = (
        P(("replica", "fsdp"), None),
        P(("replica", "fsdp"), None),
        P("replica", "fsdp", None),
        P(None, None, "fsdp"),
    )
    out_specs = (P("replica", "fsdp", None), P("fsdp", None))
    return jax.shard_map(
        on_device, mesh=mesh, in_specs=in_specs, out_specs=out_specs, check_vma=False
    )
```

```python
import functools
import math

import jax
import jax.numpy as jnp
import numpy as np
from jax import lax
from jax.experimental import pallas as pl
from jax.experimental.pallas import tpu as pltpu
from jax.sharding import PartitionSpec as P

BLOCK = 64
KEEP = 8
HALF = 256
PART = 128
DECAY = 0.9
BF16 = jnp.bfloat16
F32 = jnp.float32
VMEM = pl.BlockSpec(memory_space=pltpu.VMEM)
HBM = pl.BlockSpec(memory_space=pltpu.HBM)
SMEM = pl.BlockSpec(memory_space=pltpu.SMEM)
ANY = pl.BlockSpec(memory_space=pl.ANY)
COST = pl.CostEstimate(flops=1, bytes_accessed=1, transcendentals=0)


def paired_cosines():
    k = np.arange(BLOCK, dtype=np.float64)[:, None]
    n = np.arange(BLOCK, dtype=np.float64)[None, :]
    c = np.sqrt(np.where(k == 0, 1.0, 2.0) / BLOCK) * np.cos(np.pi * (2 * n + 1) * k / (2 * BLOCK))
    both = np.zeros((2 * BLOCK, 2 * BLOCK))
    both[:BLOCK, :BLOCK] = c
    both[BLOCK:, BLOCK:] = c
    return both.astype(np.float32)


def halves(value):
    high = value.astype(BF16)
    return high, (value - high.astype(F32)).astype(BF16)


def stacked_cosines():
    pair = paired_cosines()
    high = pair.astype(jnp.bfloat16)
    low = (pair - high.astype(np.float32)).astype(jnp.bfloat16)
    return np.concatenate([high, high, low], axis=1), np.concatenate([high, high, low], axis=0)


def products(tokens, cotangent, table, units, splits, limit, after=()):
    depth, width = cotangent.shape
    count = len(units)
    shapes = []
    for group in splits:
        if group == "parts":
            shapes += [(PART, width)] * (HALF // PART)
        else:
            shapes.append((HALF * group, width))

    def kernel(table_ref, tokens_ref, cot_ref, *refs):
        out_refs, (buffer, sems) = refs[len(after) : -2], refs[-2:]
        copies = []
        for m in range(count):
            column = pl.multiple_of(table_ref[m] * HALF, HALF)
            copies.append(pltpu.make_async_copy(tokens_ref.at[:, pl.ds(column, HALF)], buffer.at[m], sems.at[m]))
            copies[-1].start()
        at = 0
        out = 0
        for group in splits:
            for m in range(1 if group == "parts" else group):
                copies[at].wait()
                value = lax.dot_general(
                    buffer[at], cot_ref[...], (((0,), (0,)), ((), ())), preferred_element_type=F32
                )
                if group == "parts":
                    for p in range(HALF // PART):
                        out_refs[out + p][...] = value[p * PART : (p + 1) * PART]
                else:
                    out_refs[out][m * HALF : (m + 1) * HALF, :] = value
                at += 1
            out += HALF // PART if group == "parts" else 1

    return pl.pallas_call(
        kernel,
        out_shape=[jax.ShapeDtypeStruct(s, F32) for s in shapes],
        in_specs=[SMEM, HBM, VMEM] + [ANY] * len(after),
        out_specs=[VMEM] * len(shapes),
        scratch_shapes=[pltpu.VMEM((count, depth, HALF), BF16), pltpu.SemaphoreType.DMA((count,))],
        compiler_params=pltpu.CompilerParams(vmem_limit_bytes=limit),
        cost_estimate=COST,
    )(jnp.stack([table[u] for u in units]), tokens, cotangent, *after)


def combine(outputs, after=()):
    width = 512
    arrays = []
    for pieces in outputs:
        for size, terms in pieces:
            for array, _ in terms:
                if not any(array is known for known in arrays):
                    arrays.append(array)
    width = arrays[0].shape[1]
    index = lambda array: next(i for i, known in enumerate(arrays) if known is array)
    plan = [[(size, [(index(array), start) for array, start in terms]) for size, terms in pieces] for pieces in outputs]
    shapes = [(sum(size for size, _ in pieces), width) for pieces in outputs]

    def kernel(*refs):
        in_refs, out_refs = refs[: len(arrays)], refs[len(arrays) + len(after) :]
        for pieces, out_ref in zip(plan, out_refs):
            at = 0
            for size, terms in pieces:
                total = None
                for i, start in terms:
                    value = in_refs[i][start : start + size, :]
                    total = value if total is None else total + value
                out_ref[at : at + size, :] = total
                at += size

    return pl.pallas_call(
        kernel,
        out_shape=[jax.ShapeDtypeStruct(s, F32) for s in shapes],
        in_specs=[VMEM] * len(arrays) + [ANY] * len(after),
        out_specs=[VMEM] * len(shapes),
        compiler_params=pltpu.CompilerParams(vmem_limit_bytes=16 << 20),
        cost_estimate=COST,
    )(*arrays, *after)


def sort_index(kept_index, place, blocks_in_row, after=()):
    replicas, keep, blocks = kept_index.shape
    rows = blocks // blocks_in_row
    group = replicas // 2
    lanes = PART * blocks_in_row
    segments = blocks // lanes

    def kernel(place_ref, own_ref, group_ref, *refs):
        own_out, group_out = refs[len(after) :]
        taken = place_ref[3]
        lane = lax.broadcasted_iota(jnp.int32, (lanes, PART), 0)
        row = lax.broadcasted_iota(jnp.int32, (lanes, PART), 1)
        offset = lane - row * blocks_in_row
        own = jnp.concatenate([own_ref[0, :, s * lanes : (s + 1) * lanes] for s in range(segments)], axis=0)
        own = own.astype(F32).astype(BF16)
        for c in range(blocks_in_row):
            pick = jnp.where(offset == c, 1.0, 0.0).astype(BF16)
            found = jnp.dot(own, pick, preferred_element_type=F32)
            for s in range(segments):
                own_out[c, :, s * PART : (s + 1) * PART] = found[s * keep : (s + 1) * keep]
        pick = jnp.where(offset == taken, 1.0, 0.0).astype(BF16)
        for s in range(segments // 2):
            part = group_ref[:, :, s * lanes : (s + 1) * lanes].reshape(group * keep, lanes)
            found = jnp.dot(part.astype(F32).astype(BF16), pick, preferred_element_type=F32)
            group_out[:, :, s * PART : (s + 1) * PART] = found.reshape(group, keep, PART)

    return pl.pallas_call(
        kernel,
        out_shape=[
            jax.ShapeDtypeStruct((blocks_in_row, keep, rows), F32),
            jax.ShapeDtypeStruct((group, keep, rows // 2), F32),
        ],
        grid_spec=pltpu.PrefetchScalarGridSpec(
            num_scalar_prefetch=1,
            grid=(1,),
            in_specs=[
                pl.BlockSpec((1, keep, blocks), lambda i, t: (t[0], 0, 0)),
                pl.BlockSpec((group, keep, blocks // 2), lambda i, t: (t[1], 0, t[2])),
            ]
            + [ANY] * len(after),
            out_specs=[
                pl.BlockSpec((blocks_in_row, keep, rows), lambda i, t: (0, 0, 0)),
                pl.BlockSpec((group, keep, rows // 2), lambda i, t: (0, 0, 0)),
            ],
        ),
        compiler_params=pltpu.CompilerParams(vmem_limit_bytes=24 << 20),
        cost_estimate=COST,
    )(place, kept_index, kept_index, *after)


def select(parts, momentum, half, factor, chosen, forward_cos, kept):
    before = [] if kept is None else [kept]
    width = momentum.shape[1]
    pairs = width // (2 * BLOCK)

    def kernel(*refs):
        part_refs = refs[: len(parts)]
        momentum_ref, chosen_ref, cos_ref = refs[len(parts) : len(parts) + 3]
        kept_ref, moment_ref, masked_ref = refs[-3:]
        if before:
            kept_ref[2 * pairs :] = refs[len(parts) + 3][...]
        bounds = sorted({p[2] for p in parts} | {HALF})
        sums = []
        for low, high in zip(bounds[:-1], bounds[1:]):
            total = None
            for (_, start, at, size), ref in zip(parts, part_refs):
                if at <= low and at + size >= high:
                    piece = ref[start + low - at : start + high - at, :]
                    total = piece if total is None else total + piece
            sums.append(total)
        gradient = sums[0] if len(sums) == 1 else jnp.concatenate(sums, axis=0)
        moment = DECAY * momentum_ref[half * HALF : (half + 1) * HALF, :] + factor * gradient
        moment_ref[...] = moment
        high, low = halves(moment)
        frequency = lax.broadcasted_iota(jnp.int32, (BLOCK, HALF), 0).astype(F32)
        for g in range(pairs):
            columns = slice(2 * BLOCK * g, 2 * BLOCK * (g + 1))
            values = jnp.concatenate([high[:, columns], low[:, columns], high[:, columns]], axis=1)
            spectrum = lax.dot_general(cos_ref[...], values, (((1,), (1,)), ((), ())), preferred_element_type=F32)
            for s in range(2):
                own = spectrum[s * BLOCK : (s + 1) * BLOCK]
                c = 2 * g + s
                filled = jnp.zeros_like(own)
                for j in range(KEEP):
                    hit = frequency == chosen_ref[c, j : j + 1, half * HALF : (half + 1) * HALF]
                    taken = jnp.where(hit, own, 0.0)
                    kept_ref[c, j : j + 1, :] = jnp.sum(taken, axis=0, keepdims=True)
                    filled = filled + taken
                masked_ref[c * BLOCK : (c + 1) * BLOCK, :] = filled

    return pl.pallas_call(
        kernel,
        out_shape=[
            jax.ShapeDtypeStruct((2 * pairs * (1 + len(before)), KEEP, HALF), F32),
            jax.ShapeDtypeStruct((HALF, width), F32),
            jax.ShapeDtypeStruct((width, HALF), F32),
        ],
        in_specs=[VMEM] * (len(parts) + 3 + len(before)),
        out_specs=[VMEM] * 3,
        compiler_params=pltpu.CompilerParams(vmem_limit_bytes=24 << 20),
        cost_estimate=COST,
    )(*[p[0] for p in parts], momentum, chosen, forward_cos, *before)


def inverse_of(spectra, inverse_cos):
    high, low = halves(spectra)
    return lax.dot_general(
        jnp.concatenate([high, low, high], axis=0), inverse_cos, (((0,), (0,)), ((), ())), preferred_element_type=F32
    )


def remain(moments, masked, inverse_cos, after=()):
    width = moments[0].shape[1]

    def kernel(*refs):
        cos = refs[4][...]
        out_ref = refs[-1]
        for half in range(2):
            for g in range(width // PART):
                columns = slice(PART * g, PART * (g + 1))
                rebuilt = inverse_of(refs[2 + half][columns, :], cos)
                out_ref[half * HALF : (half + 1) * HALF, columns] = refs[half][:, columns] - rebuilt

    return pl.pallas_call(
        kernel,
        out_shape=jax.ShapeDtypeStruct((2 * HALF, width), F32),
        in_specs=[VMEM] * 5 + [ANY] * len(after),
        out_specs=VMEM,
        compiler_params=pltpu.CompilerParams(vmem_limit_bytes=24 << 20),
        cost_estimate=COST,
    )(*moments, *masked, inverse_cos, *after)


def spread(values, chosen, after=()):
    members, keep, rows = values.shape

    def kernel(value_ref, chosen_ref, *refs):
        out_ref = refs[-1]
        frequency = lax.broadcasted_iota(jnp.int32, (BLOCK, PART), 0).astype(F32)
        for p in range(rows // PART):
            lanes = slice(p * PART, (p + 1) * PART)

            def add(m, total):
                own = jnp.zeros((BLOCK, PART), F32)
                for j in range(keep):
                    hit = frequency == chosen_ref[m, j : j + 1, lanes]
                    own = jnp.where(hit, value_ref[m, j : j + 1, lanes], own)
                return total + own

            out_ref[:, lanes] = lax.fori_loop(0, members, add, jnp.zeros((BLOCK, PART), F32), unroll=4)

    return pl.pallas_call(
        kernel,
        out_shape=jax.ShapeDtypeStruct((BLOCK, rows), F32),
        in_specs=[VMEM] * 2 + [ANY] * len(after),
        out_specs=VMEM,
        compiler_params=pltpu.CompilerParams(vmem_limit_bytes=24 << 20),
        cost_estimate=COST,
    )(values, chosen, *after)


def double(mine, swapped, copies, after=()):
    def kernel(mine_ref, swapped_ref, *refs):
        total = mine_ref[...] + swapped_ref[...]
        for i in range(copies):
            refs[-1][i] = total

    return pl.pallas_call(
        kernel,
        out_shape=jax.ShapeDtypeStruct((copies, *mine.shape), F32),
        in_specs=[VMEM] * 2 + [ANY] * len(after),
        out_specs=VMEM,
        compiler_params=pltpu.CompilerParams(vmem_limit_bytes=16 << 20),
        cost_estimate=COST,
    )(mine, swapped, *after)


def finish(mine, other, core, inverse_cos, scale):
    width, rows = mine.shape[0] * BLOCK, mine.shape[2]

    def kernel(core_ref, mine_ref, other_ref, cos_ref, out_ref):
        cos = cos_ref[...]
        for ref, half in ((mine_ref, core_ref[0]), (other_ref, 1 - core_ref[0])):
            first = pl.multiple_of(half * rows, rows)
            for g in range(width // PART):
                spectra = jnp.concatenate([ref[2 * g], ref[2 * g + 1]], axis=0)
                out_ref[pl.ds(first, rows), PART * g : PART * (g + 1)] = scale * inverse_of(spectra, cos)

    return pl.pallas_call(
        kernel,
        out_shape=jax.ShapeDtypeStruct((2 * rows, width), F32),
        in_specs=[SMEM, VMEM, VMEM, VMEM],
        out_specs=VMEM,
        compiler_params=pltpu.CompilerParams(vmem_limit_bytes=24 << 20),
        cost_estimate=COST,
    )(core, mine, other, inverse_cos)


def on_device(tokens, cotangent, momentum, kept_index):
    nx, ny = 2, 4
    nh, nz, nc = 2, 8, 2
    width = cotangent.shape[1]
    blocks_in_row = width // BLOCK
    group_size = lax.axis_size("fsdp")
    replicas = lax.axis_size("replica")
    factor = 1.0 / math.sqrt(tokens.shape[0] * group_size)
    forward_cos, inverse_cos = (jnp.asarray(m) for m in stacked_cosines())

    f = lax.axis_index("fsdp")
    x, y = f // ny, f % ny
    r = lax.axis_index("replica")
    h, z, c = r // (nz * nc), r // nc % nz, r % nc

    up = [(i, i // ny * ny + (i + 1) % ny) for i in range(nx * ny)]
    down = [(i, i // ny * ny + (i - 1) % ny) for i in range(nx * ny)]
    across = [(i, (i + ny) % (nx * ny)) for i in range(nx * ny)]
    to_up = lambda v: lax.ppermute(v, "fsdp", up)
    to_down = lambda v: lax.ppermute(v, "fsdp", down)
    to_across = lambda v: lax.ppermute(v, "fsdp", across)

    table = {
        (dx, dy, k): ((x + dx) % nx * ny + (y + dy) % ny) * 2 + k
        for dx in range(nx)
        for dy in range(ny)
        for k in range(2)
    }
    make = functools.partial(products, tokens, cotangent, table)

    far0, far1, x21 = make(
        [(0, 2, 0), (1, 2, 0), (1, 2, 1), (1, 1, 1), (1, 3, 1)], [1, 1, 3], limit=60 << 20
    )
    a1, b1, rx21 = to_up(far0), to_down(far1), to_across(x21)
    near1, near0 = make([(1, 1, 0), (0, 3, 0)], [1, 1], limit=54 << 20, after=[far0])
    a2, b2 = to_up(near1), to_down(near0)
    last0, last1, other, own, q2, q1, q3, q0, x0 = make(
        [(0, 1, 0), (1, 3, 0), (1, 0, 0), (0, 0, 0), (0, 2, 1), (0, 1, 1), (0, 3, 1), (0, 0, 1), (1, 0, 1)],
        [1] * 9,
        limit=48 << 20,
        after=[near1],
    )
    own_chosen, group_chosen = sort_index(
        kept_index, jnp.stack([r, h, c, z]).astype(jnp.int32), blocks_in_row, after=[last0]
    )
    last0, last1 = combine([[(HALF, [(last0, 0), (a1, 0)])], [(HALF, [(last1, 0), (b1, 0)])]], after=[own_chosen])
    a3, b3 = to_up(last0), to_down(last1)
    other, own, x0 = combine(
        [[(HALF, [(other, 0), (a2, 0)])], [(HALF, [(own, 0), (b2, 0)])], [(HALF, [(x0, 0)])]], after=[last0]
    )
    rx0 = to_across(x0)
    q2a, q2b = combine(
        [[(PART, [(q2, 0), (rx21, 0)])], [(PART, [(q2, PART), (rx21, PART)])]], after=[other]
    )
    qa1, qb1 = to_up(q2a), to_down(q2b)
    other, own = combine([[(HALF, [(other, 0), (b3, 0)])], [(HALF, [(own, 0), (a3, 0)])]], after=[q2a])
    received = to_across(other)
    q1, q3 = combine(
        [
            [(PART, [(q1, 0), (rx21, HALF), (qa1, 0)]), (PART, [(q1, PART), (rx21, HALF + PART)])],
            [(PART, [(q3, 0), (rx21, 2 * HALF)]), (PART, [(q3, PART), (rx21, 2 * HALF + PART), (qb1, 0)])],
        ],
        after=[other],
    )
    qa, qb = to_up(q1), to_down(q3)

    pieces1 = [(piece, 0, 0, HALF) for piece in (q0, rx0, qa, qb)]
    pieces0 = [(piece, 0, 0, HALF) for piece in (own, received)]
    kept, moment1, masked1 = select(pieces1, momentum[0], 1, factor, own_chosen, forward_cos, None)
    kept, moment0, masked0 = select(pieces0, momentum[0], 0, factor, own_chosen, forward_cos, kept)

    groups = [[i * nz * nc + j * nc + k for k in range(nc) for j in range(nz)] for i in range(nh)]
    kept = lax.all_to_all(kept, "replica", 0, 0, tiled=True, axis_index_groups=groups)
    members = group_chosen.reshape(nz, nc, KEEP, HALF).transpose(1, 0, 2, 3).reshape(nc * nz, KEEP, HALF)
    dense = spread(kept, members)
    swapped = lax.ppermute(dense, "replica", [(i, (i + nz * nc) % replicas) for i in range(replicas)])
    rest = remain([moment0, moment1], [masked0, masked1], inverse_cos, after=[dense])
    dense = double(dense, swapped, nz, after=[rest])
    along = [[i * nz * nc + j * nc + k for j in range(nz)] for i in range(nh) for k in range(nc)]
    mine = lax.all_to_all(
        dense, "replica", 0, 0, tiled=True, axis_index_groups=along
    )
    theirs = lax.ppermute(mine, "replica", [(i, i ^ 1) for i in range(replicas)])
    update = finish(mine, theirs, c.reshape(1).astype(jnp.int32), inverse_cos, 1.0 / replicas)
    return rest[None], update


def solution(mesh):
    in_specs = (
        P(("replica", "fsdp"), None),
        P(("replica", "fsdp"), None),
        P("replica", "fsdp", None),
        P(None, None, "fsdp"),
    )
    out_specs = (P("replica", "fsdp", None), P("fsdp", None))
    return jax.shard_map(
        on_device, mesh=mesh, in_specs=in_specs, out_specs=out_specs, check_vma=False
    )
```

```python
import functools
import math

import jax
import jax.numpy as jnp
import numpy as np
from jax import lax
from jax.experimental import pallas as pl
from jax.experimental.pallas import tpu as pltpu
from jax.sharding import PartitionSpec as P

BLOCK = 64
KEEP = 8
HALF = 256
NX, NY = 2, 4
NH, NZ, NC = 2, 8, 2
PART = 128
DECAY = 0.9
BF16 = jnp.bfloat16
F32 = jnp.float32
VMEM = pl.BlockSpec(memory_space=pltpu.VMEM)
HBM = pl.BlockSpec(memory_space=pltpu.HBM)
SMEM = pl.BlockSpec(memory_space=pltpu.SMEM)
ANY = pl.BlockSpec(memory_space=pl.ANY)
COST = pl.CostEstimate(flops=1, bytes_accessed=1, transcendentals=0)


def paired_cosines():
    k = np.arange(BLOCK, dtype=np.float64)[:, None]
    n = np.arange(BLOCK, dtype=np.float64)[None, :]
    c = np.sqrt(np.where(k == 0, 1.0, 2.0) / BLOCK) * np.cos(np.pi * (2 * n + 1) * k / (2 * BLOCK))
    both = np.zeros((2 * BLOCK, 2 * BLOCK))
    both[:BLOCK, :BLOCK] = c
    both[BLOCK:, BLOCK:] = c
    return both.astype(np.float32)


def halves(value):
    high = value.astype(BF16)
    return high, (value - high.astype(F32)).astype(BF16)


def stacked_cosines():
    pair = paired_cosines()
    high = pair.astype(jnp.bfloat16)
    low = (pair - high.astype(np.float32)).astype(jnp.bfloat16)
    return np.concatenate([high, high, low], axis=1), np.concatenate([high, high, low], axis=0)


def products(tokens, cotangent, units, counts, limit, after=()):
    depth, width = cotangent.shape
    total = len(units)
    shapes = [(HALF * count, width) for count in counts]

    def kernel(tokens_ref, cot_ref, *refs):
        out_refs, (buffer, cot, sems) = refs[len(after) : -3], refs[-3:]
        f = lax.axis_index("fsdp")
        x, y = f // NY, f % NY
        copies = [pltpu.make_async_copy(cot_ref, cot, sems.at[total])]
        for m, (dx, dy, k) in enumerate(units):
            place = (x + dx) % NX * NY + (y + dy) % NY
            column = pl.multiple_of((2 * place + k) * HALF, HALF)
            copies.append(pltpu.make_async_copy(tokens_ref.at[:, pl.ds(column, HALF)], buffer.at[m], sems.at[m]))
        for copy in copies:
            copy.start()
        copies[0].wait()
        at = 0
        for count, out_ref in zip(counts, out_refs):
            for m in range(count):
                copies[1 + at].wait()
                out_ref[m * HALF : (m + 1) * HALF, :] = lax.dot_general(
                    buffer[at], cot[...], (((0,), (0,)), ((), ())), preferred_element_type=F32
                )
                at += 1

    return pl.pallas_call(
        kernel,
        out_shape=[jax.ShapeDtypeStruct(s, F32) for s in shapes],
        in_specs=[ANY, ANY] + [ANY] * len(after),
        out_specs=[VMEM] * len(shapes),
        scratch_shapes=[
            pltpu.VMEM((total, depth, HALF), BF16),
            pltpu.VMEM((depth, width), BF16),
            pltpu.SemaphoreType.DMA((total + 1,)),
        ],
        compiler_params=pltpu.CompilerParams(vmem_limit_bytes=limit),
        cost_estimate=COST,
    )(tokens, cotangent, *after)


def combine(outputs, after=()):
    arrays = []
    for pieces in outputs:
        for size, terms in pieces:
            for array, _ in terms:
                if not any(array is known for known in arrays):
                    arrays.append(array)
    width = arrays[0].shape[1]
    index = lambda array: next(i for i, known in enumerate(arrays) if known is array)
    plan = [[(size, [(index(array), start) for array, start in terms]) for size, terms in pieces] for pieces in outputs]
    shapes = [(sum(size for size, _ in pieces), width) for pieces in outputs]

    def kernel(*refs):
        in_refs, out_refs = refs[: len(arrays)], refs[len(arrays) + len(after) :]
        for pieces, out_ref in zip(plan, out_refs):
            at = 0
            for size, terms in pieces:
                total = None
                for i, start in terms:
                    value = in_refs[i][start : start + size, :]
                    total = value if total is None else total + value
                out_ref[at : at + size, :] = total
                at += size

    return pl.pallas_call(
        kernel,
        out_shape=[jax.ShapeDtypeStruct(s, F32) for s in shapes],
        in_specs=[VMEM] * len(arrays) + [ANY] * len(after),
        out_specs=[VMEM] * len(shapes),
        compiler_params=pltpu.CompilerParams(vmem_limit_bytes=16 << 20),
        cost_estimate=COST,
    )(*arrays, *after)


def sort_index(kept_index, limit, after=()):
    replicas, keep, blocks = kept_index.shape
    rows = 2 * HALF
    in_row = blocks // rows
    lanes = PART * in_row

    def kernel(index_ref, *refs):
        own_out, all_out, own_buffer, all_buffer, sems = refs[len(after) :]
        r = lax.axis_index("replica")
        h, z, c = r // (NZ * NC), r // NC % NZ, r % NC
        first = pl.multiple_of((h * NC + c) * lanes, lanes)
        copies = [
            pltpu.make_async_copy(index_ref.at[r], own_buffer, sems.at[0]),
            pltpu.make_async_copy(index_ref.at[:, :, pl.ds(first, lanes)], all_buffer, sems.at[1]),
        ]
        for copy in copies:
            copy.start()
        lane = lax.broadcasted_iota(jnp.int32, (lanes, PART), 0)
        row = lax.broadcasted_iota(jnp.int32, (lanes, PART), 1)
        offset = lane - row * in_row
        copies[0].wait()
        own = jnp.concatenate([own_buffer[:, s * lanes : (s + 1) * lanes] for s in range(rows // PART)], axis=0)
        own = own.astype(F32).astype(BF16)
        for i in range(in_row):
            pick = jnp.where(offset == i, 1.0, 0.0).astype(BF16)
            found = jnp.dot(own, pick, preferred_element_type=F32)
            for s in range(rows // PART):
                own_out[i, :, s * PART : (s + 1) * PART] = found[s * keep : (s + 1) * keep]
        copies[1].wait()
        pick = jnp.where(offset == z, 1.0, 0.0).astype(BF16)
        found = jnp.dot(
            all_buffer[...].reshape(replicas * keep, lanes).astype(F32).astype(BF16), pick, preferred_element_type=F32
        )
        all_out[...] = found.reshape(replicas, keep, PART)

    return pl.pallas_call(
        kernel,
        out_shape=[
            jax.ShapeDtypeStruct((in_row, keep, rows), F32),
            jax.ShapeDtypeStruct((replicas, keep, PART), F32),
        ],
        in_specs=[ANY] * (1 + len(after)),
        out_specs=[VMEM] * 2,
        scratch_shapes=[
            pltpu.VMEM((keep, blocks), jnp.int32),
            pltpu.VMEM((replicas, keep, lanes), jnp.int32),
            pltpu.SemaphoreType.DMA((2,)),
        ],
        compiler_params=pltpu.CompilerParams(vmem_limit_bytes=limit),
        cost_estimate=COST,
    )(kept_index, *after)


def select(parts, momentum, half, factor, chosen, forward_cos, kept, after=()):
    before = [] if kept is None else [kept]
    width = momentum.shape[1]
    pairs = width // (2 * BLOCK)

    def kernel(*refs):
        part_refs = refs[: len(parts)]
        momentum_ref, chosen_ref, cos_ref = refs[len(parts) : len(parts) + 3]
        kept_ref, moment_ref, masked_ref = refs[-3:]
        if before:
            kept_ref[: 2 * pairs * HALF // PART] = refs[len(parts) + 3][...]
        bounds = sorted({p[2] for p in parts} | {HALF})
        sums = []
        for low, high in zip(bounds[:-1], bounds[1:]):
            total = None
            for (_, start, at, size), ref in zip(parts, part_refs):
                if at <= low and at + size >= high:
                    piece = ref[start + low - at : start + high - at, :]
                    total = piece if total is None else total + piece
            sums.append(total)
        gradient = sums[0] if len(sums) == 1 else jnp.concatenate(sums, axis=0)
        moment = DECAY * momentum_ref[half * HALF : (half + 1) * HALF, :] + factor * gradient
        moment_ref[...] = moment
        high, low = halves(moment)
        frequency = lax.broadcasted_iota(jnp.int32, (BLOCK, HALF), 0).astype(F32)
        for g in range(pairs):
            columns = slice(2 * BLOCK * g, 2 * BLOCK * (g + 1))
            values = jnp.concatenate([high[:, columns], low[:, columns], high[:, columns]], axis=1)
            spectrum = lax.dot_general(cos_ref[...], values, (((1,), (1,)), ((), ())), preferred_element_type=F32)
            for s in range(2):
                own = spectrum[s * BLOCK : (s + 1) * BLOCK]
                c = 2 * g + s
                filled = jnp.zeros_like(own)
                for j in range(KEEP):
                    hit = frequency == chosen_ref[c, j : j + 1, half * HALF : (half + 1) * HALF]
                    taken = jnp.where(hit, own, 0.0)
                    kept = jnp.sum(taken, axis=0, keepdims=True)
                    for p in range(HALF // PART):
                        at = (len(before) * HALF // PART + p) * 2 * pairs + c
                        kept_ref[at, j : j + 1, :] = kept[:, p * PART : (p + 1) * PART]
                    filled = filled + taken
                masked_ref[c * BLOCK : (c + 1) * BLOCK, :] = filled

    return pl.pallas_call(
        kernel,
        out_shape=[
            jax.ShapeDtypeStruct((2 * pairs * HALF // PART * (1 + len(before)), KEEP, PART), F32),
            jax.ShapeDtypeStruct((HALF, width), F32),
            jax.ShapeDtypeStruct((width, HALF), F32),
        ],
        in_specs=[VMEM] * (len(parts) + 3 + len(before)) + [ANY] * len(after),
        out_specs=[VMEM] * 3,
        compiler_params=pltpu.CompilerParams(vmem_limit_bytes=24 << 20),
        cost_estimate=COST,
    )(*[p[0] for p in parts], momentum, chosen, forward_cos, *before, *after)


def inverse_of(spectra, inverse_cos):
    high, low = halves(spectra)
    return lax.dot_general(
        jnp.concatenate([high, low, high], axis=0), inverse_cos, (((0,), (0,)), ((), ())), preferred_element_type=F32
    )


def remain(moments, masked, inverse_cos, after=()):
    width = moments[0].shape[1]

    def kernel(*refs):
        cos = refs[4][...]
        out_ref = refs[-1]
        for half in range(2):
            for g in range(width // PART):
                columns = slice(PART * g, PART * (g + 1))
                rebuilt = inverse_of(refs[2 + half][columns, :], cos)
                out_ref[half * HALF : (half + 1) * HALF, columns] = refs[half][:, columns] - rebuilt

    return pl.pallas_call(
        kernel,
        out_shape=jax.ShapeDtypeStruct((2 * HALF, width), F32),
        grid=(1,),
        in_specs=[VMEM] * 5 + [ANY] * len(after),
        out_specs=pl.BlockSpec((2 * HALF, width), lambda i: (0, 0)),
        compiler_params=pltpu.CompilerParams(vmem_limit_bytes=24 << 20),
        cost_estimate=COST,
    )(*moments, *masked, inverse_cos, *after)


def spread(values, chosen, copies):
    members, keep, rows = values.shape

    def kernel(value_ref, chosen_ref, out_ref):
        frequency = lax.broadcasted_iota(jnp.int32, (BLOCK, rows), 0).astype(F32)

        def add(m, total):
            replica = m // (NC * NZ) * (NC * NZ) + m % NZ * NC + m // NZ % NC
            own = jnp.zeros((BLOCK, rows), F32)
            for j in range(keep):
                hit = frequency == chosen_ref[replica, j : j + 1, :]
                own = jnp.where(hit, value_ref[m, j : j + 1, :], own)
            return total + own

        total = lax.fori_loop(0, members, add, jnp.zeros((BLOCK, rows), F32), unroll=4)
        for i in range(copies):
            out_ref[i] = total

    return pl.pallas_call(
        kernel,
        out_shape=jax.ShapeDtypeStruct((copies, BLOCK, rows), F32),
        in_specs=[VMEM] * 2,
        out_specs=VMEM,
        compiler_params=pltpu.CompilerParams(vmem_limit_bytes=24 << 20),
        cost_estimate=COST,
    )(values, chosen)


def finish(mine, other, inverse_cos, scale):
    width = mine.shape[0] // NH * BLOCK

    def kernel(mine_ref, other_ref, cos_ref, out_ref):
        core = lax.axis_index("replica") % NC
        cos = cos_ref[...]
        for ref, place in ((mine_ref, core), (other_ref, 1 - core)):
            for h in range(NH):
                first = pl.multiple_of((h * NC + place) * PART, PART)
                for g in range(width // PART):
                    at = h * (width // BLOCK) + 2 * g
                    spectra = jnp.concatenate([ref[at], ref[at + 1]], axis=0)
                    out_ref[pl.ds(first, PART), PART * g : PART * (g + 1)] = scale * inverse_of(spectra, cos)

    return pl.pallas_call(
        kernel,
        out_shape=jax.ShapeDtypeStruct((NH * NC * PART, width), F32),
        in_specs=[VMEM] * 3,
        out_specs=VMEM,
        compiler_params=pltpu.CompilerParams(vmem_limit_bytes=24 << 20),
        cost_estimate=COST,
    )(mine, other, inverse_cos)


def on_device(tokens, cotangent, momentum, kept_index):
    group_size = lax.axis_size("fsdp")
    replicas = lax.axis_size("replica")
    factor = 1.0 / math.sqrt(tokens.shape[0] * group_size)
    forward_cos, inverse_cos = (jnp.asarray(m) for m in stacked_cosines())


    up = [(i, i // NY * NY + (i + 1) % NY) for i in range(NX * NY)]
    down = [(i, i // NY * NY + (i - 1) % NY) for i in range(NX * NY)]
    across = [(i, (i + NY) % (NX * NY)) for i in range(NX * NY)]
    to_up = lambda v: lax.ppermute(v, "fsdp", up)
    to_down = lambda v: lax.ppermute(v, "fsdp", down)
    to_across = lambda v: lax.ppermute(v, "fsdp", across)
    to_core = lambda v: lax.ppermute(v, "replica", [(i, i ^ 1) for i in range(replicas)])

    make = functools.partial(products, tokens, cotangent)

    (x21,) = make([(1, 2, 1), (1, 1, 1), (1, 3, 1)], [3], limit=60 << 20)
    rx21 = to_across(x21)
    far0, far1 = make([(0, 2, 0), (1, 2, 0)], [1, 1], limit=57 << 20, after=[x21])
    a1, b1 = to_up(far0), to_down(far1)
    near1, near0 = make([(1, 1, 0), (0, 3, 0)], [1, 1], limit=54 << 20, after=[far0])
    a2, b2 = to_up(near1), to_down(near0)
    last0, last1 = make([(0, 1, 0), (1, 3, 0)], [1, 1], limit=52 << 20, after=[near1])
    own_chosen, all_chosen = sort_index(kept_index, limit=50 << 20, after=[last0])
    last0, last1 = combine([[(HALF, [(last0, 0), (a1, 0)])], [(HALF, [(last1, 0), (b1, 0)])]], after=[own_chosen])
    a3, b3 = to_up(last0), to_down(last1)
    x0, other, own, q2, q1, q3, q0 = make(
        [(1, 0, 1), (1, 0, 0), (0, 0, 0), (0, 2, 1), (0, 1, 1), (0, 3, 1), (0, 0, 1)],
        [1] * 7,
        limit=48 << 20,
        after=[last0],
    )
    rx0 = to_across(x0)
    q2a, q2b = combine(
        [[(PART, [(q2, 0), (rx21, 0)])], [(PART, [(q2, PART), (rx21, PART)])]], after=[own]
    )
    qa1, qb1 = to_up(q2a), to_down(q2b)
    other, own = combine(
        [[(HALF, [(other, 0), (a2, 0), (b3, 0)])], [(HALF, [(own, 0), (b2, 0), (a3, 0)])]], after=[q2a]
    )
    received = to_across(other)
    q1, q3, q0 = combine(
        [
            [(PART, [(q1, 0), (rx21, HALF), (qa1, 0)]), (PART, [(q1, PART), (rx21, HALF + PART)])],
            [(PART, [(q3, 0), (rx21, 2 * HALF)]), (PART, [(q3, PART), (rx21, 2 * HALF + PART), (qb1, 0)])],
            [(HALF, [(q0, 0), (rx0, 0)])],
        ],
        after=[other],
    )
    qa, qb = to_up(q1), to_down(q3)

    pieces0 = [(piece, 0, 0, HALF) for piece in (own, received)]
    pieces1 = [(piece, 0, 0, HALF) for piece in (q0, qa, qb)]
    kept, moment0, masked0 = select(pieces0, momentum[0], 0, factor, own_chosen, forward_cos, None, after=[q0])
    kept, moment1, masked1 = select(pieces1, momentum[0], 1, factor, own_chosen, forward_cos, kept)

    order = [i * NZ * NC + j * NC + k for i in range(NH) for k in range(NC) for j in range(NZ)]
    kept = lax.all_to_all(kept, "replica", 0, 0, tiled=True, axis_index_groups=[order])
    summed = spread(kept, all_chosen, NH * NZ)
    cores = [[i * NZ * NC + j * NC + k for i in range(NH) for j in range(NZ)] for k in range(NC)]
    mine = lax.all_to_all(summed, "replica", 0, 0, tiled=True, axis_index_groups=cores)
    theirs = to_core(mine)
    rest = remain([moment0, moment1], [masked0, masked1], inverse_cos, after=[mine])
    update = finish(mine, theirs, inverse_cos, 1.0 / replicas)
    return rest[None], update


def solution(mesh):
    in_specs = (
        P(("replica", "fsdp"), None),
        P(("replica", "fsdp"), None),
        P("replica", "fsdp", None),
        P(None, None, "fsdp"),
    )
    out_specs = (P("replica", "fsdp", None), P("fsdp", None))
    return jax.shard_map(
        on_device, mesh=mesh, in_specs=in_specs, out_specs=out_specs, check_vma=False
    )
```

```python
import functools
import math

import jax
import jax.numpy as jnp
import numpy as np
from jax import lax
from jax.experimental import pallas as pl
from jax.experimental.pallas import tpu as pltpu
from jax.sharding import PartitionSpec as P

BLOCK = 64
KEEP = 8
HALF = 256
NX, NY = 2, 4
NH, NZ, NC = 2, 8, 2
PART = 128
DECAY = 0.9
BF16 = jnp.bfloat16
F32 = jnp.float32
VMEM = pl.BlockSpec(memory_space=pltpu.VMEM)
HBM = pl.BlockSpec(memory_space=pltpu.HBM)
SMEM = pl.BlockSpec(memory_space=pltpu.SMEM)
ANY = pl.BlockSpec(memory_space=pl.ANY)
COST = pl.CostEstimate(flops=1, bytes_accessed=1, transcendentals=0)


def paired_cosines():
    k = np.arange(BLOCK, dtype=np.float64)[:, None]
    n = np.arange(BLOCK, dtype=np.float64)[None, :]
    c = np.sqrt(np.where(k == 0, 1.0, 2.0) / BLOCK) * np.cos(np.pi * (2 * n + 1) * k / (2 * BLOCK))
    both = np.zeros((2 * BLOCK, 2 * BLOCK))
    both[:BLOCK, :BLOCK] = c
    both[BLOCK:, BLOCK:] = c
    return both.astype(np.float32)


def halves(value):
    high = value.astype(BF16)
    return high, (value - high.astype(F32)).astype(BF16)


def stacked_cosines():
    pair = paired_cosines()
    high = pair.astype(jnp.bfloat16)
    low = (pair - high.astype(np.float32)).astype(jnp.bfloat16)
    return np.concatenate([high, high, low], axis=1), np.concatenate([high, high, low], axis=0)


def products(tokens, cotangent, units, counts, limit, after=()):
    depth, width = cotangent.shape
    total = len(units)
    shapes = [(HALF * count, width) for count in counts]

    def kernel(tokens_ref, cot_ref, *refs):
        out_refs, (buffer, cot, sems) = refs[len(after) : -3], refs[-3:]
        f = lax.axis_index("fsdp")
        x, y = f // NY, f % NY
        copies = [pltpu.make_async_copy(cot_ref, cot, sems.at[total])]
        for m, (dx, dy, k) in enumerate(units):
            place = (x + dx) % NX * NY + (y + dy) % NY
            column = pl.multiple_of((2 * place + k) * HALF, HALF)
            copies.append(pltpu.make_async_copy(tokens_ref.at[:, pl.ds(column, HALF)], buffer.at[m], sems.at[m]))
        for copy in copies:
            copy.start()
        copies[0].wait()
        at = 0
        for count, out_ref in zip(counts, out_refs):
            for m in range(count):
                copies[1 + at].wait()
                out_ref[m * HALF : (m + 1) * HALF, :] = lax.dot_general(
                    buffer[at], cot[...], (((0,), (0,)), ((), ())), preferred_element_type=F32
                )
                at += 1

    return pl.pallas_call(
        kernel,
        out_shape=[jax.ShapeDtypeStruct(s, F32) for s in shapes],
        in_specs=[ANY, ANY] + [ANY] * len(after),
        out_specs=[VMEM] * len(shapes),
        scratch_shapes=[
            pltpu.VMEM((total, depth, HALF), BF16),
            pltpu.VMEM((depth, width), BF16),
            pltpu.SemaphoreType.DMA((total + 1,)),
        ],
        compiler_params=pltpu.CompilerParams(vmem_limit_bytes=limit),
        cost_estimate=COST,
    )(tokens, cotangent, *after)


def combine(outputs, after=()):
    arrays = []
    for pieces in outputs:
        for size, terms in pieces:
            for array, _ in terms:
                if not any(array is known for known in arrays):
                    arrays.append(array)
    width = arrays[0].shape[1]
    index = lambda array: next(i for i, known in enumerate(arrays) if known is array)
    plan = [[(size, [(index(array), start) for array, start in terms]) for size, terms in pieces] for pieces in outputs]
    shapes = [(sum(size for size, _ in pieces), width) for pieces in outputs]

    def kernel(*refs):
        in_refs, out_refs = refs[: len(arrays)], refs[len(arrays) + len(after) :]
        for pieces, out_ref in zip(plan, out_refs):
            at = 0
            for size, terms in pieces:
                total = None
                for i, start in terms:
                    value = in_refs[i][start : start + size, :]
                    total = value if total is None else total + value
                out_ref[at : at + size, :] = total
                at += size

    return pl.pallas_call(
        kernel,
        out_shape=[jax.ShapeDtypeStruct(s, F32) for s in shapes],
        in_specs=[VMEM] * len(arrays) + [ANY] * len(after),
        out_specs=[VMEM] * len(shapes),
        compiler_params=pltpu.CompilerParams(vmem_limit_bytes=16 << 20),
        cost_estimate=COST,
    )(*arrays, *after)


def sort_index(kept_index, limit, after=()):
    replicas, keep, blocks = kept_index.shape
    rows = 2 * HALF
    in_row = blocks // rows
    lanes = PART * in_row

    def kernel(index_ref, *refs):
        own_out, all_out, own_buffer, all_buffer, sems = refs[len(after) :]
        r = lax.axis_index("replica")
        h, z, c = r // (NZ * NC), r // NC % NZ, r % NC
        first = pl.multiple_of((h * NC + c) * lanes, lanes)
        copies = [
            pltpu.make_async_copy(index_ref.at[r], own_buffer, sems.at[0]),
            pltpu.make_async_copy(index_ref.at[:, :, pl.ds(first, lanes)], all_buffer, sems.at[1]),
        ]
        for copy in copies:
            copy.start()
        lane = lax.broadcasted_iota(jnp.int32, (lanes, PART), 0)
        row = lax.broadcasted_iota(jnp.int32, (lanes, PART), 1)
        offset = lane - row * in_row
        copies[0].wait()
        own = jnp.concatenate([own_buffer[:, s * lanes : (s + 1) * lanes] for s in range(rows // PART)], axis=0)
        own = own.astype(F32).astype(BF16)
        for i in range(in_row):
            pick = jnp.where(offset == i, 1.0, 0.0).astype(BF16)
            found = jnp.dot(own, pick, preferred_element_type=F32)
            for s in range(rows // PART):
                own_out[i, :, s * PART : (s + 1) * PART] = found[s * keep : (s + 1) * keep]
        copies[1].wait()
        pick = jnp.where(offset == z, 1.0, 0.0).astype(BF16)
        found = jnp.dot(
            all_buffer[...].reshape(replicas * keep, lanes).astype(F32).astype(BF16), pick, preferred_element_type=F32
        )
        all_out[...] = found.reshape(replicas, keep, PART)

    return pl.pallas_call(
        kernel,
        out_shape=[
            jax.ShapeDtypeStruct((in_row, keep, rows), F32),
            jax.ShapeDtypeStruct((replicas, keep, PART), F32),
        ],
        in_specs=[ANY] * (1 + len(after)),
        out_specs=[VMEM] * 2,
        scratch_shapes=[
            pltpu.VMEM((keep, blocks), jnp.int32),
            pltpu.VMEM((replicas, keep, lanes), jnp.int32),
            pltpu.SemaphoreType.DMA((2,)),
        ],
        compiler_params=pltpu.CompilerParams(vmem_limit_bytes=limit),
        cost_estimate=COST,
    )(kept_index, *after)


def select(parts, momentum, half, factor, chosen, forward_cos, kept, after=()):
    before = [] if kept is None else [kept]
    width = momentum.shape[1]
    pairs = width // (2 * BLOCK)

    def kernel(*refs):
        part_refs = refs[: len(parts)]
        momentum_ref, chosen_ref, cos_ref = refs[len(parts) : len(parts) + 3]
        kept_ref, moment_ref, masked_ref = refs[-3:]
        if before:
            kept_ref[: 2 * pairs * HALF // PART] = refs[len(parts) + 3][...]
        bounds = sorted({p[2] for p in parts} | {HALF})
        sums = []
        for low, high in zip(bounds[:-1], bounds[1:]):
            total = None
            for (_, start, at, size), ref in zip(parts, part_refs):
                if at <= low and at + size >= high:
                    piece = ref[start + low - at : start + high - at, :]
                    total = piece if total is None else total + piece
            sums.append(total)
        gradient = sums[0] if len(sums) == 1 else jnp.concatenate(sums, axis=0)
        moment = DECAY * momentum_ref[half * HALF : (half + 1) * HALF, :] + factor * gradient
        moment_ref[...] = moment
        high, low = halves(moment)
        frequency = lax.broadcasted_iota(jnp.int32, (BLOCK, HALF), 0).astype(F32)
        for g in range(pairs):
            columns = slice(2 * BLOCK * g, 2 * BLOCK * (g + 1))
            values = jnp.concatenate([high[:, columns], low[:, columns], high[:, columns]], axis=1)
            spectrum = lax.dot_general(cos_ref[...], values, (((1,), (1,)), ((), ())), preferred_element_type=F32)
            for s in range(2):
                own = spectrum[s * BLOCK : (s + 1) * BLOCK]
                c = 2 * g + s
                filled = jnp.zeros_like(own)
                for j in range(KEEP):
                    hit = frequency == chosen_ref[c, j : j + 1, half * HALF : (half + 1) * HALF]
                    taken = jnp.where(hit, own, 0.0)
                    kept = jnp.sum(taken, axis=0, keepdims=True)
                    for p in range(HALF // PART):
                        at = (len(before) * HALF // PART + p) * 2 * pairs + c
                        kept_ref[at, j : j + 1, :] = kept[:, p * PART : (p + 1) * PART]
                    filled = filled + taken
                masked_ref[c * BLOCK : (c + 1) * BLOCK, :] = filled

    return pl.pallas_call(
        kernel,
        out_shape=[
            jax.ShapeDtypeStruct((2 * pairs * HALF // PART * (1 + len(before)), KEEP, PART), F32),
            jax.ShapeDtypeStruct((HALF, width), F32),
            jax.ShapeDtypeStruct((width, HALF), F32),
        ],
        in_specs=[VMEM] * (len(parts) + 3 + len(before)) + [ANY] * len(after),
        out_specs=[VMEM] * 3,
        compiler_params=pltpu.CompilerParams(vmem_limit_bytes=24 << 20),
        cost_estimate=COST,
    )(*[p[0] for p in parts], momentum, chosen, forward_cos, *before, *after)


def inverse_of(spectra, inverse_cos):
    high, low = halves(spectra)
    return lax.dot_general(
        jnp.concatenate([high, low, high], axis=0), inverse_cos, (((0,), (0,)), ((), ())), preferred_element_type=F32
    )


def remain(moments, masked, inverse_cos, after=()):
    width = moments[0].shape[1]

    def kernel(*refs):
        cos = refs[4][...]
        out_ref = refs[-1]
        for half in range(2):
            for g in range(width // PART):
                columns = slice(PART * g, PART * (g + 1))
                rebuilt = inverse_of(refs[2 + half][columns, :], cos)
                out_ref[half * HALF : (half + 1) * HALF, columns] = refs[half][:, columns] - rebuilt

    return pl.pallas_call(
        kernel,
        out_shape=jax.ShapeDtypeStruct((2 * HALF, width), F32),
        grid=(1,),
        in_specs=[VMEM] * 5 + [ANY] * len(after),
        out_specs=pl.BlockSpec((2 * HALF, width), lambda i: (0, 0)),
        compiler_params=pltpu.CompilerParams(vmem_limit_bytes=24 << 20),
        cost_estimate=COST,
    )(*moments, *masked, inverse_cos, *after)


def spread(values, chosen, copies):
    members, keep, rows = values.shape

    def kernel(value_ref, chosen_ref, out_ref):
        frequency = lax.broadcasted_iota(jnp.int32, (BLOCK, rows), 0).astype(F32)

        def add(m, total):
            replica = m // (NC * NZ) * (NC * NZ) + m % NZ * NC + m // NZ % NC
            own = jnp.zeros((BLOCK, rows), F32)
            for j in range(keep):
                hit = frequency == chosen_ref[replica, j : j + 1, :]
                own = jnp.where(hit, value_ref[m, j : j + 1, :], own)
            return total + own

        total = lax.fori_loop(0, members, add, jnp.zeros((BLOCK, rows), F32), unroll=4)
        for i in range(copies):
            out_ref[i] = total

    return pl.pallas_call(
        kernel,
        out_shape=jax.ShapeDtypeStruct((copies, BLOCK, rows), F32),
        in_specs=[VMEM] * 2,
        out_specs=VMEM,
        compiler_params=pltpu.CompilerParams(vmem_limit_bytes=24 << 20),
        cost_estimate=COST,
    )(values, chosen)


def finish(mine, other, inverse_cos, scale):
    width = mine.shape[0] // NH * BLOCK

    def kernel(mine_ref, other_ref, cos_ref, out_ref):
        core = lax.axis_index("replica") % NC
        cos = cos_ref[...]
        for ref, place in ((mine_ref, core), (other_ref, 1 - core)):
            for h in range(NH):
                first = pl.multiple_of((h * NC + place) * PART, PART)
                for g in range(width // PART):
                    at = h * (width // BLOCK) + 2 * g
                    spectra = jnp.concatenate([ref[at], ref[at + 1]], axis=0)
                    out_ref[pl.ds(first, PART), PART * g : PART * (g + 1)] = scale * inverse_of(spectra, cos)

    return pl.pallas_call(
        kernel,
        out_shape=jax.ShapeDtypeStruct((NH * NC * PART, width), F32),
        in_specs=[VMEM] * 3,
        out_specs=VMEM,
        compiler_params=pltpu.CompilerParams(vmem_limit_bytes=24 << 20),
        cost_estimate=COST,
    )(mine, other, inverse_cos)


def on_device(tokens, cotangent, momentum, kept_index):
    group_size = lax.axis_size("fsdp")
    replicas = lax.axis_size("replica")
    factor = 1.0 / math.sqrt(tokens.shape[0] * group_size)
    forward_cos, inverse_cos = (jnp.asarray(m) for m in stacked_cosines())


    up = [(i, i // NY * NY + (i + 1) % NY) for i in range(NX * NY)]
    down = [(i, i // NY * NY + (i - 1) % NY) for i in range(NX * NY)]
    across = [(i, (i + NY) % (NX * NY)) for i in range(NX * NY)]
    to_up = lambda v: lax.ppermute(v, "fsdp", up)
    to_down = lambda v: lax.ppermute(v, "fsdp", down)
    to_across = lambda v: lax.ppermute(v, "fsdp", across)
    to_core = lambda v: lax.ppermute(v, "replica", [(i, i ^ 1) for i in range(replicas)])

    make = functools.partial(products, tokens, cotangent)

    x21, far0, far1 = make([(1, 2, 1), (1, 1, 1), (1, 3, 1), (0, 2, 0), (1, 2, 0)], [3, 1, 1], limit=60 << 20)
    rx21 = to_across(x21)
    a1, b1 = to_up(far0), to_down(far1)
    near1, near0 = make([(1, 1, 0), (0, 3, 0)], [1, 1], limit=54 << 20, after=[far0])
    a2, b2 = to_up(near1), to_down(near0)
    last0, last1 = make([(0, 1, 0), (1, 3, 0)], [1, 1], limit=52 << 20, after=[near1])
    own_chosen, all_chosen = sort_index(kept_index, limit=50 << 20, after=[last0])
    last0, last1 = combine([[(HALF, [(last0, 0), (a1, 0)])], [(HALF, [(last1, 0), (b1, 0)])]], after=[own_chosen])
    a3, b3 = to_up(last0), to_down(last1)
    x0, other, own, q2, q1, q3, q0 = make(
        [(1, 0, 1), (1, 0, 0), (0, 0, 0), (0, 2, 1), (0, 1, 1), (0, 3, 1), (0, 0, 1)],
        [1] * 7,
        limit=48 << 20,
        after=[last0],
    )
    rx0 = to_across(x0)
    q2a, q2b = combine(
        [[(PART, [(q2, 0), (rx21, 0)])], [(PART, [(q2, PART), (rx21, PART)])]], after=[own]
    )
    qa1, qb1 = to_up(q2a), to_down(q2b)
    other, own = combine(
        [[(HALF, [(other, 0), (a2, 0), (b3, 0)])], [(HALF, [(own, 0), (b2, 0), (a3, 0)])]], after=[q2a]
    )
    received = to_across(other)
    (q1,) = combine(
        [[(PART, [(q1, 0), (rx21, HALF), (qa1, 0)]), (PART, [(q1, PART), (rx21, HALF + PART)])]], after=[other]
    )
    qa = to_up(q1)
    q3, q0 = combine(
        [
            [(PART, [(q3, 0), (rx21, 2 * HALF)]), (PART, [(q3, PART), (rx21, 2 * HALF + PART), (qb1, 0)])],
            [(HALF, [(q0, 0), (rx0, 0)])],
        ],
        after=[q1],
    )
    qb = to_down(q3)

    pieces0 = [(piece, 0, 0, HALF) for piece in (own, received)]
    pieces1 = [(piece, 0, 0, HALF) for piece in (q0, qa, qb)]
    kept, moment0, masked0 = select(pieces0, momentum[0], 0, factor, own_chosen, forward_cos, None, after=[q0])
    kept, moment1, masked1 = select(pieces1, momentum[0], 1, factor, own_chosen, forward_cos, kept)

    order = [i * NZ * NC + j * NC + k for i in range(NH) for k in range(NC) for j in range(NZ)]
    kept = lax.all_to_all(kept, "replica", 0, 0, tiled=True, axis_index_groups=[order])
    summed = spread(kept, all_chosen, NH * NZ)
    cores = [[i * NZ * NC + j * NC + k for i in range(NH) for j in range(NZ)] for k in range(NC)]
    mine = lax.all_to_all(summed, "replica", 0, 0, tiled=True, axis_index_groups=cores)
    theirs = to_core(mine)
    rest = remain([moment0, moment1], [masked0, masked1], inverse_cos, after=[mine])
    update = finish(mine, theirs, inverse_cos, 1.0 / replicas)
    return rest[None], update


def solution(mesh):
    in_specs = (
        P(("replica", "fsdp"), None),
        P(("replica", "fsdp"), None),
        P("replica", "fsdp", None),
        P(None, None, "fsdp"),
    )
    out_specs = (P("replica", "fsdp", None), P("fsdp", None))
    return jax.shard_map(
        on_device, mesh=mesh, in_specs=in_specs, out_specs=out_specs, check_vma=False
    )
```

```python
import functools
import math

import jax
import jax.numpy as jnp
import numpy as np
from jax import lax
from jax.experimental import pallas as pl
from jax.experimental.pallas import tpu as pltpu
from jax.sharding import PartitionSpec as P

BLOCK = 64
KEEP = 8
HALF = 256
NX, NY = 2, 4
NH, NZ, NC = 2, 8, 2
PART = 128
DECAY = 0.9
BF16 = jnp.bfloat16
F32 = jnp.float32
VMEM = pl.BlockSpec(memory_space=pltpu.VMEM)
HBM = pl.BlockSpec(memory_space=pltpu.HBM)
SMEM = pl.BlockSpec(memory_space=pltpu.SMEM)
ANY = pl.BlockSpec(memory_space=pl.ANY)
COST = pl.CostEstimate(flops=1, bytes_accessed=1, transcendentals=0)


def paired_cosines():
    k = np.arange(BLOCK, dtype=np.float64)[:, None]
    n = np.arange(BLOCK, dtype=np.float64)[None, :]
    c = np.sqrt(np.where(k == 0, 1.0, 2.0) / BLOCK) * np.cos(np.pi * (2 * n + 1) * k / (2 * BLOCK))
    both = np.zeros((2 * BLOCK, 2 * BLOCK))
    both[:BLOCK, :BLOCK] = c
    both[BLOCK:, BLOCK:] = c
    return both.astype(np.float32)


def halves(value):
    high = value.astype(BF16)
    return high, (value - high.astype(F32)).astype(BF16)


def stacked_cosines():
    pair = paired_cosines()
    high = pair.astype(jnp.bfloat16)
    low = (pair - high.astype(np.float32)).astype(jnp.bfloat16)
    return np.concatenate([high, high, low], axis=1), np.concatenate([high, high, low], axis=0)


def products(tokens, cotangent, units, counts, limit, after=()):
    depth, width = cotangent.shape
    total = len(units)
    shapes = [(HALF * count, width) for count in counts]

    def kernel(tokens_ref, cot_ref, *refs):
        out_refs, (buffer, cot, sems) = refs[len(after) : -3], refs[-3:]
        f = lax.axis_index("fsdp")
        x, y = f // NY, f % NY
        copies = [pltpu.make_async_copy(cot_ref, cot, sems.at[total])]
        for m, (dx, dy, k) in enumerate(units):
            place = (x + dx) % NX * NY + (y + dy) % NY
            column = pl.multiple_of((2 * place + k) * HALF, HALF)
            copies.append(pltpu.make_async_copy(tokens_ref.at[:, pl.ds(column, HALF)], buffer.at[m], sems.at[m]))
        for copy in copies:
            copy.start()
        copies[0].wait()
        at = 0
        for count, out_ref in zip(counts, out_refs):
            for m in range(count):
                copies[1 + at].wait()
                out_ref[m * HALF : (m + 1) * HALF, :] = lax.dot_general(
                    buffer[at], cot[...], (((0,), (0,)), ((), ())), preferred_element_type=F32
                )
                at += 1

    return pl.pallas_call(
        kernel,
        out_shape=[jax.ShapeDtypeStruct(s, F32) for s in shapes],
        in_specs=[ANY, ANY] + [ANY] * len(after),
        out_specs=[VMEM] * len(shapes),
        scratch_shapes=[
            pltpu.VMEM((total, depth, HALF), BF16),
            pltpu.VMEM((depth, width), BF16),
            pltpu.SemaphoreType.DMA((total + 1,)),
        ],
        compiler_params=pltpu.CompilerParams(vmem_limit_bytes=limit),
        cost_estimate=COST,
    )(tokens, cotangent, *after)


def combine(outputs, after=()):
    arrays = []
    for pieces in outputs:
        for size, terms in pieces:
            for array, _ in terms:
                if not any(array is known for known in arrays):
                    arrays.append(array)
    width = arrays[0].shape[1]
    index = lambda array: next(i for i, known in enumerate(arrays) if known is array)
    plan = [[(size, [(index(array), start) for array, start in terms]) for size, terms in pieces] for pieces in outputs]
    shapes = [(sum(size for size, _ in pieces), width) for pieces in outputs]

    def kernel(*refs):
        in_refs, out_refs = refs[: len(arrays)], refs[len(arrays) + len(after) :]
        for pieces, out_ref in zip(plan, out_refs):
            at = 0
            for size, terms in pieces:
                total = None
                for i, start in terms:
                    value = in_refs[i][start : start + size, :]
                    total = value if total is None else total + value
                out_ref[at : at + size, :] = total
                at += size

    return pl.pallas_call(
        kernel,
        out_shape=[jax.ShapeDtypeStruct(s, F32) for s in shapes],
        in_specs=[VMEM] * len(arrays) + [ANY] * len(after),
        out_specs=[VMEM] * len(shapes),
        compiler_params=pltpu.CompilerParams(vmem_limit_bytes=16 << 20),
        cost_estimate=COST,
    )(*arrays, *after)


def sort_index(kept_index, limit, after=()):
    replicas, keep, blocks = kept_index.shape
    rows = 2 * HALF
    in_row = blocks // rows
    lanes = PART * in_row

    def kernel(index_ref, *refs):
        own_out, all_out, own_buffer, all_buffer, sems = refs[len(after) :]
        r = lax.axis_index("replica")
        h, z, c = r // (NZ * NC), r // NC % NZ, r % NC
        first = pl.multiple_of((h * NC + c) * lanes, lanes)
        copies = [
            pltpu.make_async_copy(index_ref.at[r], own_buffer, sems.at[0]),
            pltpu.make_async_copy(index_ref.at[:, :, pl.ds(first, lanes)], all_buffer, sems.at[1]),
        ]
        for copy in copies:
            copy.start()
        lane = lax.broadcasted_iota(jnp.int32, (lanes, PART), 0)
        row = lax.broadcasted_iota(jnp.int32, (lanes, PART), 1)
        offset = lane - row * in_row
        copies[0].wait()
        own = jnp.concatenate([own_buffer[:, s * lanes : (s + 1) * lanes] for s in range(rows // PART)], axis=0)
        own = own.astype(F32).astype(BF16)
        for i in range(in_row):
            pick = jnp.where(offset == i, 1.0, 0.0).astype(BF16)
            found = jnp.dot(own, pick, preferred_element_type=F32)
            for s in range(rows // PART):
                own_out[i, :, s * PART : (s + 1) * PART] = found[s * keep : (s + 1) * keep]
        copies[1].wait()
        pick = jnp.where(offset == z, 1.0, 0.0).astype(BF16)
        found = jnp.dot(
            all_buffer[...].reshape(replicas * keep, lanes).astype(F32).astype(BF16), pick, preferred_element_type=F32
        )
        all_out[...] = found.reshape(replicas, keep, PART)

    return pl.pallas_call(
        kernel,
        out_shape=[
            jax.ShapeDtypeStruct((in_row, keep, rows), F32),
            jax.ShapeDtypeStruct((replicas, keep, PART), F32),
        ],
        in_specs=[ANY] * (1 + len(after)),
        out_specs=[VMEM] * 2,
        scratch_shapes=[
            pltpu.VMEM((keep, blocks), jnp.int32),
            pltpu.VMEM((replicas, keep, lanes), jnp.int32),
            pltpu.SemaphoreType.DMA((2,)),
        ],
        compiler_params=pltpu.CompilerParams(vmem_limit_bytes=limit),
        cost_estimate=COST,
    )(kept_index, *after)


def select(parts, momentum, half, factor, chosen, forward_cos, kept, after=()):
    before = [] if kept is None else [kept]
    width = momentum.shape[1]
    pairs = width // (2 * BLOCK)

    def kernel(*refs):
        part_refs = refs[: len(parts)]
        momentum_ref, chosen_ref, cos_ref = refs[len(parts) : len(parts) + 3]
        kept_ref, moment_ref, masked_ref = refs[-3:]
        if before:
            kept_ref[: 2 * pairs * HALF // PART] = refs[len(parts) + 3][...]
        bounds = sorted({p[2] for p in parts} | {HALF})
        sums = []
        for low, high in zip(bounds[:-1], bounds[1:]):
            total = None
            for (_, start, at, size), ref in zip(parts, part_refs):
                if at <= low and at + size >= high:
                    piece = ref[start + low - at : start + high - at, :]
                    total = piece if total is None else total + piece
            sums.append(total)
        gradient = sums[0] if len(sums) == 1 else jnp.concatenate(sums, axis=0)
        moment = DECAY * momentum_ref[half * HALF : (half + 1) * HALF, :] + factor * gradient
        moment_ref[...] = moment
        high, low = halves(moment)
        frequency = lax.broadcasted_iota(jnp.int32, (BLOCK, HALF), 0).astype(F32)
        for g in range(pairs):
            columns = slice(2 * BLOCK * g, 2 * BLOCK * (g + 1))
            values = jnp.concatenate([high[:, columns], low[:, columns], high[:, columns]], axis=1)
            spectrum = lax.dot_general(cos_ref[...], values, (((1,), (1,)), ((), ())), preferred_element_type=F32)
            for s in range(2):
                own = spectrum[s * BLOCK : (s + 1) * BLOCK]
                c = 2 * g + s
                filled = jnp.zeros_like(own)
                for j in range(KEEP):
                    hit = frequency == chosen_ref[c, j : j + 1, half * HALF : (half + 1) * HALF]
                    taken = jnp.where(hit, own, 0.0)
                    kept = jnp.sum(taken, axis=0, keepdims=True)
                    for p in range(HALF // PART):
                        at = (len(before) * 2 * pairs + c) * (HALF // PART) + p
                        kept_ref[at, j : j + 1, :] = kept[:, p * PART : (p + 1) * PART]
                    filled = filled + taken
                masked_ref[c * BLOCK : (c + 1) * BLOCK, :] = filled

    return pl.pallas_call(
        kernel,
        out_shape=[
            jax.ShapeDtypeStruct((2 * pairs * HALF // PART * (1 + len(before)), KEEP, PART), F32),
            jax.ShapeDtypeStruct((HALF, width), F32),
            jax.ShapeDtypeStruct((width, HALF), F32),
        ],
        in_specs=[VMEM] * (len(parts) + 3 + len(before)) + [ANY] * len(after),
        out_specs=[VMEM] * 3,
        compiler_params=pltpu.CompilerParams(vmem_limit_bytes=24 << 20),
        cost_estimate=COST,
    )(*[p[0] for p in parts], momentum, chosen, forward_cos, *before, *after)


def inverse_of(spectra, inverse_cos):
    high, low = halves(spectra)
    return lax.dot_general(
        jnp.concatenate([high, low, high], axis=0), inverse_cos, (((0,), (0,)), ((), ())), preferred_element_type=F32
    )


def remain(moments, masked, inverse_cos, after=()):
    width = moments[0].shape[1]

    def kernel(*refs):
        cos = refs[4][...]
        out_ref = refs[-1]
        for half in range(2):
            for g in range(width // PART):
                columns = slice(PART * g, PART * (g + 1))
                rebuilt = inverse_of(refs[2 + half][columns, :], cos)
                out_ref[half * HALF : (half + 1) * HALF, columns] = refs[half][:, columns] - rebuilt

    return pl.pallas_call(
        kernel,
        out_shape=jax.ShapeDtypeStruct((2 * HALF, width), F32),
        grid=(1,),
        in_specs=[VMEM] * 5 + [ANY] * len(after),
        out_specs=pl.BlockSpec((2 * HALF, width), lambda i: (0, 0)),
        compiler_params=pltpu.CompilerParams(vmem_limit_bytes=24 << 20),
        cost_estimate=COST,
    )(*moments, *masked, inverse_cos, *after)


def spread(values, chosen, copies):
    members, keep, rows = values.shape

    def kernel(value_ref, chosen_ref, out_ref):
        frequency = lax.broadcasted_iota(jnp.int32, (BLOCK, rows), 0).astype(F32)

        def add(m, total):
            own = jnp.zeros((BLOCK, rows), F32)
            for j in range(keep):
                hit = frequency == chosen_ref[m, j : j + 1, :]
                own = jnp.where(hit, value_ref[m, j : j + 1, :], own)
            return total + own

        total = lax.fori_loop(0, members, add, jnp.zeros((BLOCK, rows), F32), unroll=4)
        for i in range(copies):
            out_ref[i] = total

    return pl.pallas_call(
        kernel,
        out_shape=jax.ShapeDtypeStruct((copies, BLOCK, rows), F32),
        in_specs=[VMEM] * 2,
        out_specs=VMEM,
        compiler_params=pltpu.CompilerParams(vmem_limit_bytes=24 << 20),
        cost_estimate=COST,
    )(values, chosen)


def finish(mine, other, inverse_cos, scale):
    width = mine.shape[0] // NH * BLOCK

    def kernel(mine_ref, other_ref, cos_ref, out_ref):
        core = lax.axis_index("replica") % NC
        cos = cos_ref[...]
        for ref, place in ((mine_ref, core), (other_ref, 1 - core)):
            for h in range(NH):
                first = pl.multiple_of((h * NC + place) * PART, PART)
                for g in range(width // PART):
                    at = h * (width // BLOCK) + 2 * g
                    spectra = jnp.concatenate([ref[at], ref[at + 1]], axis=0)
                    out_ref[pl.ds(first, PART), PART * g : PART * (g + 1)] = scale * inverse_of(spectra, cos)

    return pl.pallas_call(
        kernel,
        out_shape=jax.ShapeDtypeStruct((NH * NC * PART, width), F32),
        in_specs=[VMEM] * 3,
        out_specs=VMEM,
        compiler_params=pltpu.CompilerParams(vmem_limit_bytes=24 << 20),
        cost_estimate=COST,
    )(mine, other, inverse_cos)


def on_device(tokens, cotangent, momentum, kept_index):
    group_size = lax.axis_size("fsdp")
    replicas = lax.axis_size("replica")
    factor = 1.0 / math.sqrt(tokens.shape[0] * group_size)
    forward_cos, inverse_cos = (jnp.asarray(m) for m in stacked_cosines())


    up = [(i, i // NY * NY + (i + 1) % NY) for i in range(NX * NY)]
    down = [(i, i // NY * NY + (i - 1) % NY) for i in range(NX * NY)]
    across = [(i, (i + NY) % (NX * NY)) for i in range(NX * NY)]
    to_up = lambda v: lax.ppermute(v, "fsdp", up)
    to_down = lambda v: lax.ppermute(v, "fsdp", down)
    to_across = lambda v: lax.ppermute(v, "fsdp", across)
    to_core = lambda v: lax.ppermute(v, "replica", [(i, i ^ 1) for i in range(replicas)])

    make = functools.partial(products, tokens, cotangent)

    x21, far0, far1 = make([(1, 2, 1), (1, 1, 1), (1, 3, 1), (0, 2, 0), (1, 2, 0)], [3, 1, 1], limit=60 << 20)
    rx21 = to_across(x21)
    a1, b1 = to_up(far0), to_down(far1)
    near1, near0 = make([(1, 1, 0), (0, 3, 0)], [1, 1], limit=54 << 20, after=[far0])
    a2, b2 = to_up(near1), to_down(near0)
    last0, last1 = make([(0, 1, 0), (1, 3, 0)], [1, 1], limit=52 << 20, after=[near1])
    own_chosen, all_chosen = sort_index(kept_index, limit=50 << 20, after=[last0])
    last0, last1 = combine([[(HALF, [(last0, 0), (a1, 0)])], [(HALF, [(last1, 0), (b1, 0)])]], after=[own_chosen])
    a3, b3 = to_up(last0), to_down(last1)
    x0, other, own, q2, q1, q3, q0 = make(
        [(1, 0, 1), (1, 0, 0), (0, 0, 0), (0, 2, 1), (0, 1, 1), (0, 3, 1), (0, 0, 1)],
        [1] * 7,
        limit=48 << 20,
        after=[last0],
    )
    rx0 = to_across(x0)
    q2a, q2b = combine(
        [[(PART, [(q2, 0), (rx21, 0)])], [(PART, [(q2, PART), (rx21, PART)])]], after=[own]
    )
    qa1, qb1 = to_up(q2a), to_down(q2b)
    other, own = combine(
        [[(HALF, [(other, 0), (a2, 0), (b3, 0)])], [(HALF, [(own, 0), (b2, 0), (a3, 0)])]], after=[q2a]
    )
    received = to_across(other)
    (q3a,) = combine([[(PART, [(q3, 0), (rx21, 2 * HALF)])]], after=[other])
    qba = to_down(q3a)
    (q1,) = combine(
        [[(PART, [(q1, 0), (rx21, HALF), (qa1, 0)]), (PART, [(q1, PART), (rx21, HALF + PART)])]], after=[q3a]
    )
    qa = to_up(q1)
    q3b, q0 = combine(
        [[(PART, [(q3, PART), (rx21, 2 * HALF + PART), (qb1, 0)])], [(HALF, [(q0, 0), (rx0, 0)])]], after=[q1]
    )
    qbb = to_down(q3b)

    pieces0 = [(piece, 0, 0, HALF) for piece in (own, received)]
    pieces1 = [(q0, 0, 0, HALF), (qa, 0, 0, HALF), (qba, 0, 0, PART), (qbb, 0, PART, PART)]
    kept, moment0, masked0 = select(pieces0, momentum[0], 0, factor, own_chosen, forward_cos, None, after=[q0])
    kept, moment1, masked1 = select(pieces1, momentum[0], 1, factor, own_chosen, forward_cos, kept)

    kept = lax.all_to_all(kept, "replica", 0, 0, tiled=True)
    summed = spread(kept, all_chosen, NH * NZ)
    cores = [[i * NZ * NC + j * NC + k for i in range(NH) for j in range(NZ)] for k in range(NC)]
    mine = lax.all_to_all(summed, "replica", 0, 0, tiled=True, axis_index_groups=cores)
    theirs = to_core(mine)
    rest = remain([moment0, moment1], [masked0, masked1], inverse_cos, after=[mine])
    update = finish(mine, theirs, inverse_cos, 1.0 / replicas)
    return rest[None], update


def solution(mesh):
    in_specs = (
        P(("replica", "fsdp"), None),
        P(("replica", "fsdp"), None),
        P("replica", "fsdp", None),
        P(None, None, "fsdp"),
    )
    out_specs = (P("replica", "fsdp", None), P("fsdp", None))
    return jax.shard_map(
        on_device, mesh=mesh, in_specs=in_specs, out_specs=out_specs, check_vma=False
    )
```

```python
import functools
import math

import jax
import jax.numpy as jnp
import numpy as np
from jax import lax
from jax.experimental import pallas as pl
from jax.experimental.pallas import tpu as pltpu
from jax.sharding import PartitionSpec as P

BLOCK = 64
KEEP = 8
HALF = 256
NX, NY = 2, 4
NH, NZ, NC = 2, 8, 2
PART = 128
DECAY = 0.9
BF16 = jnp.bfloat16
F32 = jnp.float32
VMEM = pl.BlockSpec(memory_space=pltpu.VMEM)
HBM = pl.BlockSpec(memory_space=pltpu.HBM)
SMEM = pl.BlockSpec(memory_space=pltpu.SMEM)
ANY = pl.BlockSpec(memory_space=pl.ANY)
COST = pl.CostEstimate(flops=1, bytes_accessed=1, transcendentals=0)


def paired_cosines():
    k = np.arange(BLOCK, dtype=np.float64)[:, None]
    n = np.arange(BLOCK, dtype=np.float64)[None, :]
    c = np.sqrt(np.where(k == 0, 1.0, 2.0) / BLOCK) * np.cos(np.pi * (2 * n + 1) * k / (2 * BLOCK))
    both = np.zeros((2 * BLOCK, 2 * BLOCK))
    both[:BLOCK, :BLOCK] = c
    both[BLOCK:, BLOCK:] = c
    return both.astype(np.float32)


def halves(value):
    high = value.astype(BF16)
    return high, (value - high.astype(F32)).astype(BF16)


def stacked_cosines():
    pair = paired_cosines()
    high = pair.astype(jnp.bfloat16)
    low = (pair - high.astype(np.float32)).astype(jnp.bfloat16)
    return np.concatenate([high, high, low], axis=1), np.concatenate([high, high, low], axis=0)


def products(tokens, cotangent, units, counts, limit, after=()):
    depth, width = cotangent.shape
    total = len(units)
    shapes = [(HALF * count, width) for count in counts]

    def kernel(tokens_ref, cot_ref, *refs):
        out_refs, (buffer, cot, sems) = refs[len(after) : -3], refs[-3:]
        f = lax.axis_index("fsdp")
        x, y = f // NY, f % NY
        copies = [pltpu.make_async_copy(cot_ref, cot, sems.at[total])]
        for m, (dx, dy, k) in enumerate(units):
            place = (x + dx) % NX * NY + (y + dy) % NY
            column = pl.multiple_of((2 * place + k) * HALF, HALF)
            copies.append(pltpu.make_async_copy(tokens_ref.at[:, pl.ds(column, HALF)], buffer.at[m], sems.at[m]))
        for copy in copies:
            copy.start()
        copies[0].wait()
        at = 0
        for count, out_ref in zip(counts, out_refs):
            for m in range(count):
                copies[1 + at].wait()
                out_ref[m * HALF : (m + 1) * HALF, :] = lax.dot_general(
                    buffer[at], cot[...], (((0,), (0,)), ((), ())), preferred_element_type=F32
                )
                at += 1

    return pl.pallas_call(
        kernel,
        out_shape=[jax.ShapeDtypeStruct(s, F32) for s in shapes],
        in_specs=[ANY, ANY] + [ANY] * len(after),
        out_specs=[VMEM] * len(shapes),
        scratch_shapes=[
            pltpu.VMEM((total, depth, HALF), BF16),
            pltpu.VMEM((depth, width), BF16),
            pltpu.SemaphoreType.DMA((total + 1,)),
        ],
        compiler_params=pltpu.CompilerParams(vmem_limit_bytes=limit),
        cost_estimate=COST,
    )(tokens, cotangent, *after)


def combine(outputs, after=()):
    arrays = []
    for pieces in outputs:
        for size, terms in pieces:
            for array, _ in terms:
                if not any(array is known for known in arrays):
                    arrays.append(array)
    width = arrays[0].shape[1]
    index = lambda array: next(i for i, known in enumerate(arrays) if known is array)
    plan = [[(size, [(index(array), start) for array, start in terms]) for size, terms in pieces] for pieces in outputs]
    shapes = [(sum(size for size, _ in pieces), width) for pieces in outputs]

    def kernel(*refs):
        in_refs, out_refs = refs[: len(arrays)], refs[len(arrays) + len(after) :]
        for pieces, out_ref in zip(plan, out_refs):
            at = 0
            for size, terms in pieces:
                total = None
                for i, start in terms:
                    value = in_refs[i][start : start + size, :]
                    total = value if total is None else total + value
                out_ref[at : at + size, :] = total
                at += size

    return pl.pallas_call(
        kernel,
        out_shape=[jax.ShapeDtypeStruct(s, F32) for s in shapes],
        in_specs=[VMEM] * len(arrays) + [ANY] * len(after),
        out_specs=[VMEM] * len(shapes),
        compiler_params=pltpu.CompilerParams(vmem_limit_bytes=16 << 20),
        cost_estimate=COST,
    )(*arrays, *after)


def sort_index(kept_index, limit, after=()):
    replicas, keep, blocks = kept_index.shape
    rows = 2 * HALF
    in_row = blocks // rows
    lanes = PART * in_row

    def kernel(index_ref, *refs):
        own_out, all_out, own_buffer, all_buffer, sems = refs[len(after) :]
        r = lax.axis_index("replica")
        h, z, c = r // (NZ * NC), r // NC % NZ, r % NC
        first = pl.multiple_of((h * NC + c) * lanes, lanes)
        copies = [
            pltpu.make_async_copy(index_ref.at[r], own_buffer, sems.at[0]),
            pltpu.make_async_copy(index_ref.at[:, :, pl.ds(first, lanes)], all_buffer, sems.at[1]),
        ]
        for copy in copies:
            copy.start()
        lane = lax.broadcasted_iota(jnp.int32, (lanes, PART), 0)
        row = lax.broadcasted_iota(jnp.int32, (lanes, PART), 1)
        offset = lane - row * in_row
        copies[0].wait()
        own = jnp.concatenate([own_buffer[:, s * lanes : (s + 1) * lanes] for s in range(rows // PART)], axis=0)
        own = own.astype(F32).astype(BF16)
        for i in range(in_row):
            pick = jnp.where(offset == i, 1.0, 0.0).astype(BF16)
            found = jnp.dot(own, pick, preferred_element_type=F32)
            for s in range(rows // PART):
                own_out[i, :, s * PART : (s + 1) * PART] = found[s * keep : (s + 1) * keep]
        copies[1].wait()
        pick = jnp.where(offset == z, 1.0, 0.0).astype(BF16)
        found = jnp.dot(
            all_buffer[...].reshape(replicas * keep, lanes).astype(F32).astype(BF16), pick, preferred_element_type=F32
        )
        all_out[...] = found.reshape(replicas, keep, PART)

    return pl.pallas_call(
        kernel,
        out_shape=[
            jax.ShapeDtypeStruct((in_row, keep, rows), F32),
            jax.ShapeDtypeStruct((replicas, keep, PART), F32),
        ],
        in_specs=[ANY] * (1 + len(after)),
        out_specs=[VMEM] * 2,
        scratch_shapes=[
            pltpu.VMEM((keep, blocks), jnp.int32),
            pltpu.VMEM((replicas, keep, lanes), jnp.int32),
            pltpu.SemaphoreType.DMA((2,)),
        ],
        compiler_params=pltpu.CompilerParams(vmem_limit_bytes=limit),
        cost_estimate=COST,
    )(kept_index, *after)


def select(parts, momentum, half, factor, chosen, forward_cos, kept, after=()):
    before = [] if kept is None else [kept]
    width = momentum.shape[1]
    pairs = width // (2 * BLOCK)

    def kernel(*refs):
        part_refs = refs[: len(parts)]
        momentum_ref, chosen_ref, cos_ref = refs[len(parts) : len(parts) + 3]
        kept_ref, moment_ref, masked_ref = refs[-3:]
        if before:
            kept_ref[: 2 * pairs * HALF // PART] = refs[len(parts) + 3][...]
        bounds = sorted({p[2] for p in parts} | {HALF})
        sums = []
        for low, high in zip(bounds[:-1], bounds[1:]):
            total = None
            for (_, start, at, size), ref in zip(parts, part_refs):
                if at <= low and at + size >= high:
                    piece = ref[start + low - at : start + high - at, :]
                    total = piece if total is None else total + piece
            sums.append(total)
        gradient = sums[0] if len(sums) == 1 else jnp.concatenate(sums, axis=0)
        moment = DECAY * momentum_ref[half * HALF : (half + 1) * HALF, :] + factor * gradient
        moment_ref[...] = moment
        high, low = halves(moment)
        frequency = lax.broadcasted_iota(jnp.int32, (BLOCK, HALF), 0).astype(F32)
        for g in range(pairs):
            columns = slice(2 * BLOCK * g, 2 * BLOCK * (g + 1))
            values = jnp.concatenate([high[:, columns], low[:, columns], high[:, columns]], axis=1)
            spectrum = lax.dot_general(cos_ref[...], values, (((1,), (1,)), ((), ())), preferred_element_type=F32)
            for s in range(2):
                own = spectrum[s * BLOCK : (s + 1) * BLOCK]
                c = 2 * g + s
                filled = jnp.zeros_like(own)
                for j in range(KEEP):
                    hit = frequency == chosen_ref[c, j : j + 1, half * HALF : (half + 1) * HALF]
                    taken = jnp.where(hit, own, 0.0)
                    kept = jnp.sum(taken, axis=0, keepdims=True)
                    for p in range(HALF // PART):
                        at = (len(before) * 2 * pairs + c) * (HALF // PART) + p
                        kept_ref[at, j : j + 1, :] = kept[:, p * PART : (p + 1) * PART]
                    filled = filled + taken
                masked_ref[c * BLOCK : (c + 1) * BLOCK, :] = filled

    return pl.pallas_call(
        kernel,
        out_shape=[
            jax.ShapeDtypeStruct((2 * pairs * HALF // PART * (1 + len(before)), KEEP, PART), F32),
            jax.ShapeDtypeStruct((HALF, width), F32),
            jax.ShapeDtypeStruct((width, HALF), F32),
        ],
        in_specs=[VMEM] * (len(parts) + 3 + len(before)) + [ANY] * len(after),
        out_specs=[VMEM] * 3,
        compiler_params=pltpu.CompilerParams(vmem_limit_bytes=24 << 20),
        cost_estimate=COST,
    )(*[p[0] for p in parts], momentum, chosen, forward_cos, *before, *after)


def inverse_of(spectra, inverse_cos):
    high, low = halves(spectra)
    return lax.dot_general(
        jnp.concatenate([high, low, high], axis=0), inverse_cos, (((0,), (0,)), ((), ())), preferred_element_type=F32
    )


def remain(moments, masked, inverse_cos, after=()):
    width = moments[0].shape[1]

    def kernel(*refs):
        cos = refs[4][...]
        out_ref = refs[-1]
        for half in range(2):
            for g in range(width // PART):
                columns = slice(PART * g, PART * (g + 1))
                rebuilt = inverse_of(refs[2 + half][columns, :], cos)
                out_ref[half * HALF : (half + 1) * HALF, columns] = refs[half][:, columns] - rebuilt

    return pl.pallas_call(
        kernel,
        out_shape=jax.ShapeDtypeStruct((2 * HALF, width), F32),
        grid=(1,),
        in_specs=[VMEM] * 5 + [ANY] * len(after),
        out_specs=pl.BlockSpec((2 * HALF, width), lambda i: (0, 0)),
        compiler_params=pltpu.CompilerParams(vmem_limit_bytes=24 << 20),
        cost_estimate=COST,
    )(*moments, *masked, inverse_cos, *after)


def spread(values, chosen, copies):
    members, keep, rows = values.shape

    def kernel(value_ref, chosen_ref, out_ref):
        frequency = lax.broadcasted_iota(jnp.int32, (BLOCK, rows), 0).astype(F32)

        def add(m, total):
            own = jnp.zeros((BLOCK, rows), F32)
            for j in range(keep):
                hit = frequency == chosen_ref[m, j : j + 1, :]
                own = jnp.where(hit, value_ref[m, j : j + 1, :], own)
            return total + own

        total = lax.fori_loop(0, members, add, jnp.zeros((BLOCK, rows), F32), unroll=4)
        for i in range(copies):
            out_ref[i] = total

    return pl.pallas_call(
        kernel,
        out_shape=jax.ShapeDtypeStruct((copies, BLOCK, rows), F32),
        in_specs=[VMEM] * 2,
        out_specs=VMEM,
        compiler_params=pltpu.CompilerParams(vmem_limit_bytes=24 << 20),
        cost_estimate=COST,
    )(values, chosen)


def finish(mine, other, inverse_cos, scale):
    width = mine.shape[0] // NH * BLOCK

    def kernel(mine_ref, other_ref, cos_ref, out_ref, made, sems):
        core = lax.axis_index("replica") % NC
        cos = cos_ref[...]
        copies = []
        for ref, place in ((mine_ref, core), (other_ref, 1 - core)):
            for h in range(NH):
                part = len(copies)
                for g in range(width // PART):
                    at = h * (width // BLOCK) + 2 * g
                    spectra = jnp.concatenate([ref[at], ref[at + 1]], axis=0)
                    made[part, :, PART * g : PART * (g + 1)] = scale * inverse_of(spectra, cos)
                first = pl.multiple_of((h * NC + place) * PART, PART)
                copies.append(pltpu.make_async_copy(made.at[part], out_ref.at[pl.ds(first, PART), :], sems.at[part]))
                copies[-1].start()
        for copy in copies:
            copy.wait()

    return pl.pallas_call(
        kernel,
        out_shape=jax.ShapeDtypeStruct((NH * NC * PART, width), F32),
        in_specs=[VMEM] * 3,
        out_specs=ANY,
        scratch_shapes=[pltpu.VMEM((NH * NC, PART, width), F32), pltpu.SemaphoreType.DMA((NH * NC,))],
        compiler_params=pltpu.CompilerParams(vmem_limit_bytes=24 << 20),
        cost_estimate=COST,
    )(mine, other, inverse_cos)


def on_device(tokens, cotangent, momentum, kept_index):
    group_size = lax.axis_size("fsdp")
    replicas = lax.axis_size("replica")
    factor = 1.0 / math.sqrt(tokens.shape[0] * group_size)
    forward_cos, inverse_cos = (jnp.asarray(m) for m in stacked_cosines())


    up = [(i, i // NY * NY + (i + 1) % NY) for i in range(NX * NY)]
    down = [(i, i // NY * NY + (i - 1) % NY) for i in range(NX * NY)]
    across = [(i, (i + NY) % (NX * NY)) for i in range(NX * NY)]
    to_up = lambda v: lax.ppermute(v, "fsdp", up)
    to_down = lambda v: lax.ppermute(v, "fsdp", down)
    to_across = lambda v: lax.ppermute(v, "fsdp", across)
    to_core = lambda v: lax.ppermute(v, "replica", [(i, i ^ 1) for i in range(replicas)])

    make = functools.partial(products, tokens, cotangent)

    x21, far0, far1 = make([(1, 2, 1), (1, 1, 1), (1, 3, 1), (0, 2, 0), (1, 2, 0)], [3, 1, 1], limit=60 << 20)
    rx21 = to_across(x21)
    a1, b1 = to_up(far0), to_down(far1)
    near1, near0 = make([(1, 1, 0), (0, 3, 0)], [1, 1], limit=54 << 20, after=[far0])
    a2, b2 = to_up(near1), to_down(near0)
    last0, last1 = make([(0, 1, 0), (1, 3, 0)], [1, 1], limit=52 << 20, after=[near1])
    own_chosen, all_chosen = sort_index(kept_index, limit=50 << 20, after=[last0])
    last0, last1 = combine([[(HALF, [(last0, 0), (a1, 0)])], [(HALF, [(last1, 0), (b1, 0)])]], after=[own_chosen])
    a3, b3 = to_up(last0), to_down(last1)
    x0, other, own, q2, q1, q3, q0 = make(
        [(1, 0, 1), (1, 0, 0), (0, 0, 0), (0, 2, 1), (0, 1, 1), (0, 3, 1), (0, 0, 1)],
        [1] * 7,
        limit=48 << 20,
        after=[last0],
    )
    rx0 = to_across(x0)
    q2a, q2b = combine(
        [[(PART, [(q2, 0), (rx21, 0)])], [(PART, [(q2, PART), (rx21, PART)])]], after=[own]
    )
    qa1, qb1 = to_up(q2a), to_down(q2b)
    other, own = combine(
        [[(HALF, [(other, 0), (a2, 0), (b3, 0)])], [(HALF, [(own, 0), (b2, 0), (a3, 0)])]], after=[q2a]
    )
    received = to_across(other)
    (q3a,) = combine([[(PART, [(q3, 0), (rx21, 2 * HALF)])]], after=[other])
    qba = to_down(q3a)
    (q1,) = combine(
        [[(PART, [(q1, 0), (rx21, HALF), (qa1, 0)]), (PART, [(q1, PART), (rx21, HALF + PART)])]], after=[q3a]
    )
    qa = to_up(q1)
    q3b, q0 = combine(
        [[(PART, [(q3, PART), (rx21, 2 * HALF + PART), (qb1, 0)])], [(HALF, [(q0, 0), (rx0, 0)])]], after=[q1]
    )
    qbb = to_down(q3b)

    pieces0 = [(piece, 0, 0, HALF) for piece in (own, received)]
    pieces1 = [(q0, 0, 0, HALF), (qa, 0, 0, HALF), (qba, 0, 0, PART), (qbb, 0, PART, PART)]
    kept, moment0, masked0 = select(pieces0, momentum[0], 0, factor, own_chosen, forward_cos, None, after=[q0])
    kept, moment1, masked1 = select(pieces1, momentum[0], 1, factor, own_chosen, forward_cos, kept)

    kept = lax.all_to_all(kept, "replica", 0, 0, tiled=True)
    summed = spread(kept, all_chosen, NH * NZ)
    cores = [[i * NZ * NC + j * NC + k for i in range(NH) for j in range(NZ)] for k in range(NC)]
    mine = lax.all_to_all(summed, "replica", 0, 0, tiled=True, axis_index_groups=cores)
    theirs = to_core(mine)
    rest = remain([moment0, moment1], [masked0, masked1], inverse_cos, after=[mine])
    update = finish(mine, theirs, inverse_cos, 1.0 / replicas)
    return rest[None], update


def solution(mesh):
    in_specs = (
        P(("replica", "fsdp"), None),
        P(("replica", "fsdp"), None),
        P("replica", "fsdp", None),
        P(None, None, "fsdp"),
    )
    out_specs = (P("replica", "fsdp", None), P("fsdp", None))
    return jax.shard_map(
        on_device, mesh=mesh, in_specs=in_specs, out_specs=out_specs, check_vma=False
    )
```
